512 devices in a mesh: cam: 64 (over y, x, core), pt: 8 (over z).
Axes of the slice: x: 4, y: 8, z: 8, core: 2. Of those that a mesh axis runs over, the one named last changes fastest.
Arguments:
- solution: float32 [9, 16384], P(None, 'cam'), may hold values from -0.3125 to 0.3125
- residual: float32 [9, 16384], P(None, 'cam'), may hold values from -6 to 6
- direction: float32 [9, 16384], P(None, 'cam'), may hold values from -6 to 6
- cam_damping: float32 [9, 16384], P(None, 'cam'), may hold values from 4 to 40
- precond: float32 [81, 16384], P(None, 'cam'), may hold values from -0.07 to 3, as said below
- pt_damping: float32 [1048576], P(('cam', 'pt')), may hold values from 0.5 to 2
- cam_jac: float32 [32768, 18, 128], P(('cam', 'pt')), may hold values from -2 to 2
- pt_jac: float32 [32768, 6, 128], P(('cam', 'pt')), may hold values from -6 to 6
- cam_ids: int32 [32768, 128], P(('cam', 'pt')), may hold values from 0 to 255
- point_ids: int32 [32768, 128], P(('cam', 'pt')), may hold values from 0 to 2047
- owners: int32 [32768, 1], P(('cam', 'pt')), may hold values from 0 to 63; in each aligned block of 64 rows (0 to 63, 64 to 127, ...) at most 2 rows name the same one
- valid_counts: int32 [32768], P(('cam', 'pt')), may hold values from 32 to 128, as said below
Outputs:
- new_solution: float32 [9, 16384], P(None, 'cam')
- new_residual: float32 [9, 16384], P(None, 'cam')
- new_direction: float32 [9, 16384], P(None, 'cam')
The draws below stay inside these ranges and needn't reach their ends.
Inputs may be any that keep to these rules, and one draw needn't show every extreme that they name: `owners`: among the 64 tiles of one device no owner appears more than 2 times. `valid_counts`: every eighth tile is full. `precond`: each 9x9 block is symmetric with a positive, strictly dominant diagonal.
All inputs are finite; a program needn't handle non-finite values.
Results may differ from the reference program's by a relative error of at most 0.0003.
Values sent between devices are 32-bit elements; how exact they have to be, the bound alone decides.
No kernel may reach another device: no remote copies, remote signals or barrier semaphores. Data moves between devices by JAX's collectives and lax.ppermute only.
A program may use at most 64 MiB of HBM per device.

```python
import math
import jax
import jax.numpy as jnp
import numpy as np

TILE = 128
TILES_DEV = 64
CAM_DEV = 256
PT_DEV = 2048
MOST = 2
OWNERS = 64
TILES = 32768
CAMS = 16384
POINTS = 1048576
N_PT = 8


def draw_valid_counts(key, part):
    key = jax.random.fold_in(key, 5)
    counts = jax.random.randint(key, (TILES,), 32, TILE + 1)
    index = jnp.arange(TILES, dtype=jnp.int32)
    return jnp.where(index % 8 == 0, TILE, counts).astype(jnp.int32)


def draw_precond(key, part):
    key = jax.random.fold_in(key, 7)
    key_diag, key_off = jax.random.split(key)
    low, high, spread = (0.5, 2.0, 0.06)
    unit = jax.random.uniform(key_diag, (9, CAMS), jnp.float32)
    diagonal = low * jnp.exp(unit * jnp.log(high / low))
    offdiag = jax.random.uniform(key_off, (9, 9, CAMS), jnp.float32, -spread, spread)
    symmetric = (offdiag + offdiag.transpose(1, 0, 2)) * 0.5
    identity = jnp.eye(9, dtype=jnp.float32)[:, :, None]
    blocks = symmetric * (1.0 - identity) + identity * diagonal[None, :, :]
    return blocks.reshape(81, CAMS)


def plant(result, stream_key, smallest, largest):
    index_at = [jax.random.randint(jax.random.fold_in(stream_key, axis), (), 0, length) for axis, length in enumerate(result.shape)]
    longest = result.shape.index(max(result.shape))
    next_to = index_at[:longest] + [(index_at[longest] + 1) % result.shape[longest]] + index_at[longest + 1:]
    return result.at[tuple(index_at)].set(smallest).at[tuple(next_to)].set(largest)


def steps_of(own_key, dims, cuts, least, high):
    def one(position, blocks):
        draws = jax.random.uniform(jax.random.fold_in(jax.random.fold_in(own_key, 6), position), (blocks,), jnp.float32, least / len(cuts), high / len(cuts))
        return jnp.repeat(jnp.exp(draws), dims[position] // blocks).reshape((-1,) + (1,) * (len(dims) - position - 1))

    factor_of = one(*cuts[0])
    for cut in cuts[1:]:
        factor_of = factor_of * one(*cut)
    return factor_of


def deal_out(stream_key, own, number, rows, count, top, most, lean):
    order = jax.random.permutation(stream_key, count)
    crowded, usual = load_shares(count, rows * top, most, lean, True), load_shares(count, rows * top, most, lean, False)
    places = jnp.arange(count)

    def named(sizes, turn):
        used = int((sizes > 0).sum())
        fixed = max(1, used // 4)
        moved = fixed + (places - fixed + turn * (used - fixed)) % max(1, count - fixed)
        return jnp.zeros((count,), jnp.int32).at[order[jnp.where(places < fixed, places, moved)]].set(jnp.asarray(sizes, jnp.int32))

    sizes = jnp.where(number % 4 == 0, named(crowded, number // 4), named(usual, number - number // 4 - 1))
    mixed = jax.random.permutation(jax.random.fold_in(own, 3), count)
    giver, sink = mixed[0:count // 2 * 2:2], mixed[1:count // 2 * 2:2]
    room = jnp.minimum(sizes[giver] - 1, most - sizes[sink]) // 2
    room = jnp.where((giver == order[0]) | (sink == order[0]) | (sizes[sink] == 0), 0, jnp.maximum(room, 0))
    moved = jax.random.randint(jax.random.fold_in(own, 4), (count // 2,), 0, 1 << 20) % (room + 1)
    sizes = sizes.at[giver].add(-moved).at[sink].add(moved)
    members = jnp.searchsorted(jnp.cumsum(sizes), jnp.arange(rows * top), side="right").astype(jnp.int32)
    grid = members.reshape(top, rows).T
    grid = grid[jax.random.permutation(jax.random.fold_in(own, 1), rows)]
    turn = jax.random.randint(jax.random.fold_in(own, 2), (rows, 1), 0, top)
    return jnp.take_along_axis(grid, (jnp.arange(top)[None, :] + turn) % top, axis=1)


def load_shares(number_of, total, most, skew, full):
    loads = [(1 << 20) // math.isqrt(standing ** skew) + 1 for standing in range(1, number_of + 1)]
    largest = most if full else min(most, max(-(-total // number_of), total * loads[0] // sum(loads)))
    least = 1 if total - largest >= number_of - 1 else 0
    given, spare = [largest] + [least] * (number_of - 1), total - largest - least * (number_of - 1)
    while spare > 0:
        candidates = [i for i in range(1, number_of) if given[i] < largest] or [i for i in range(1, number_of) if given[i] < most]
        whole, remaining = sum([loads[i] for i in candidates]), spare
        for i in candidates:
            addition = min(most - given[i], max(1, remaining * loads[i] // whole), spare)
            given[i] = given[i] + addition
            spare = spare - addition
    return np.array(given)


def bell_draw(stream_key, dims, scale, most, pieces=(), kind=jnp.bfloat16):
    drawn = scale * jax.random.normal(stream_key, dims, jnp.float32)
    if pieces:
        drawn = drawn * steps_of(stream_key, dims, pieces, -0.22, 0.18)
    return jnp.clip(drawn, -most, most).astype(kind)


def setup_inputs(seed: int = 0) -> dict:
    arg_keys = jax.random.split(jax.random.key(seed), 13)
    solution = bell_draw(arg_keys[0], (9, CAMS), 0.02, 0.3125, ((1, 64),), jnp.float32)
    residual = bell_draw(arg_keys[1], (9, CAMS), 1.0, 6.0, ((1, 64),), jnp.float32)
    direction = bell_draw(arg_keys[2], (9, CAMS), 1.0, 6.0, ((1, 64),), jnp.float32)
    cam_damping = jnp.clip(jnp.exp(math.log(40.0) - 2.3025851 * jax.random.uniform(arg_keys[3], (9, CAMS), jnp.float32) ** steps_of(arg_keys[3], (9, CAMS), ((1, 64),), -0.2, 0.2)), 4.0, 40.0)
    precond = draw_precond(jax.random.fold_in(arg_keys[12], 71), 0)
    pt_damping = jnp.clip(jnp.exp(math.log(2.0) - 1.3862944 * jax.random.uniform(arg_keys[5], (POINTS,), jnp.float32) ** steps_of(arg_keys[5], (POINTS,), ((0, 512),), -0.2, 0.2)), 0.5, 2.0)
    cam_jac = bell_draw(arg_keys[6], (TILES, 18, TILE), 9 ** -0.5, 2.0, ((0, 512),), jnp.float32)
    pt_jac = bell_draw(arg_keys[7], (TILES, 6, TILE), 1.0, 6.0, ((0, 512),), jnp.float32)
    cam_ids = plant(jax.random.randint(arg_keys[8], (TILES, TILE), 0, CAM_DEV), jax.random.fold_in(arg_keys[8], 1), 0, CAM_DEV - 1).astype(jnp.int32)
    point_ids = plant(jax.random.randint(arg_keys[9], (TILES, TILE), 0, PT_DEV), jax.random.fold_in(arg_keys[9], 1), 0, PT_DEV - 1).astype(jnp.int32)
    owners_keys = jax.random.split(jax.random.fold_in(arg_keys[10], 1), TILES // TILES_DEV)
    owners_turns = jax.random.permutation(jax.random.fold_in(arg_keys[10], 3), TILES // TILES_DEV)
    owners = jax.vmap(lambda own, number: deal_out(jax.random.fold_in(arg_keys[10], 2), own, number, TILES_DEV, OWNERS, 1, MOST, 2))(owners_keys, owners_turns).reshape((TILES, 1))
    valid_counts = draw_valid_counts(jax.random.fold_in(arg_keys[12], 71), 0)
    return {"solution": solution, "residual": residual, "direction": direction, "cam_damping": cam_damping, "precond": precond, "pt_damping": pt_damping, "cam_jac": cam_jac, "pt_jac": pt_jac, "cam_ids": cam_ids, "point_ids": point_ids, "owners": owners, "valid_counts": valid_counts}


def project(cam_jac, gathered, valid):
    first = jnp.sum(cam_jac[:, 0:9] * gathered, axis=1)
    second = jnp.sum(cam_jac[:, 9:18] * gathered, axis=1)
    return jnp.stack([first, second], axis=1) * valid[:, None, :]


def point_terms(jacobian, errors):
    return jnp.stack([jacobian[:, column] * errors[:, 0] + jacobian[:, 3 + column] * errors[:, 1] for column in range(3)], axis=1)


def normal_terms(jacobian):
    pairs = [(0, 0), (0, 1), (0, 2), (1, 1), (1, 2), (2, 2)]
    return jnp.stack([jacobian[:, first] * jacobian[:, second] + jacobian[:, 3 + first] * jacobian[:, 3 + second] for first, second in pairs], axis=1)


def solve_points(rhs, normal, damping):
    upper_aa = normal[0] + damping
    upper_ab = normal[1]
    upper_ac = normal[2]
    upper_bb = normal[3] + damping
    upper_bc = normal[4]
    upper_cc = normal[5] + damping
    minor_aa = upper_bb * upper_cc - upper_bc * upper_bc
    minor_ab = upper_ac * upper_bc - upper_ab * upper_cc
    minor_ac = upper_ab * upper_bc - upper_ac * upper_bb
    minor_bb = upper_aa * upper_cc - upper_ac * upper_ac
    minor_bc = upper_ab * upper_ac - upper_aa * upper_bc
    minor_cc = upper_aa * upper_bb - upper_ab * upper_ab
    determ = upper_aa * minor_aa + upper_ab * minor_ab + upper_ac * minor_ac
    first = (minor_aa * rhs[0] + minor_ab * rhs[1] + minor_ac * rhs[2]) / determ
    second = (minor_ab * rhs[0] + minor_bb * rhs[1] + minor_bc * rhs[2]) / determ
    third = (minor_ac * rhs[0] + minor_bc * rhs[1] + minor_cc * rhs[2]) / determ
    return jnp.stack([first, second, third], axis=0)


def apply_points(jacobian, values):
    return jnp.stack([sum(jacobian[:, 3 * row + column] * values[:, column] for column in range(3)) for row in range(2)], axis=1)


def camera_terms(cam_jac, errors):
    return jnp.stack([cam_jac[:, column] * errors[:, 0] + cam_jac[:, 9 + column] * errors[:, 1] for column in range(9)], axis=1)


def precondition(precond, vector):
    return jnp.sum(precond.reshape(9, 9, -1) * vector[None], axis=1)


def reference(solution, residual, direction, cam_damping, precond, pt_damping, cam_jac, pt_jac, cam_ids, point_ids, owners, valid_counts):
    tile_device = jnp.arange(TILES, dtype=jnp.int32) // TILES_DEV
    cluster = tile_device // N_PT
    group = tile_device % N_PT
    global_cam = (cluster * CAM_DEV)[:, None] + cam_ids
    global_point = ((owners[:, 0] * N_PT + group) * PT_DEV)[:, None] + point_ids
    valid = (jnp.arange(TILE, dtype=jnp.int32)[None, :] < valid_counts[:, None]).astype(jnp.float32)
    first_z = precondition(precond, residual)
    product_rz = jnp.sum(residual * first_z)
    gathered = jnp.take(direction, global_cam, axis=1).transpose(1, 0, 2)
    errors = project(cam_jac, gathered, valid)
    masked_jac = pt_jac * valid[:, None, :]
    stacked = jnp.concatenate([point_terms(masked_jac, errors), normal_terms(masked_jac)], axis=1)
    flat_terms = stacked.transpose(1, 0, 2).reshape(9, -1)
    sums = jnp.zeros((9, POINTS), jnp.float32).at[:, global_point.reshape(-1)].add(flat_terms)
    point_sol = solve_points(sums[:3], sums[3:], pt_damping)
    tile_sol = jnp.take(point_sol, global_point, axis=1).transpose(1, 0, 2)
    remain = errors - apply_points(masked_jac, tile_sol)
    cam_terms = camera_terms(cam_jac, remain).transpose(1, 0, 2).reshape(9, -1)
    image = cam_damping * direction + jnp.zeros((9, CAMS), jnp.float32).at[:, global_cam.reshape(-1)].add(cam_terms)
    alpha = product_rz / jnp.sum(direction * image)
    new_solution = solution + alpha * direction
    new_residual = residual - alpha * image
    next_z = precondition(precond, new_residual)
    product_next = jnp.sum(new_residual * next_z)
    new_direction = next_z + (product_next / product_rz) * direction
    return new_solution, new_residual, new_direction
```

```python
import functools

import jax
import jax.numpy as jnp
from jax import lax
from jax.experimental import pallas as pl
from jax.experimental.pallas import tpu as pltpu
from jax.sharding import PartitionSpec as P

LANES = 128
PER_OWNER = 2
SLOT_ROWS = 9
TERM_ROWS = 32
GROUP = 8
POINT_LOW = 256
PARTS = 3

f32 = jnp.float32
bf16 = jnp.bfloat16
i32 = jnp.int32


def split(value):
    high = value.astype(bf16).astype(f32)
    rest = value - high
    middle = rest.astype(bf16).astype(f32)
    low = (rest - middle).astype(bf16).astype(f32)
    return high, middle, low


def lookup(table, index):
    return jnp.take_along_axis(table, index, axis=1, mode="promise_in_bounds")


def contract(left, right):
    return lax.dot_general(left, right, (((1,), (1,)), ((), ())), preferred_element_type=f32)


def pack_kernel(
    owners, counts, direction, cam_ids, cam_jac, pt_jac, point_ids, payload, slots, seen, table
):
    tiles, width = cam_ids.shape
    owner_count = seen.shape[0]
    payload[...] = jnp.zeros(payload.shape, f32)

    @pl.loop(0, owner_count)
    def _(index):
        seen[index] = 0

    table[0:9, :] = direction[...]
    table[9:18, :] = direction[...]
    table[18:24, :] = jnp.zeros((6, table.shape[1]), f32)
    tables = [
        [table[8 * g : 8 * g + 8, LANES * c : LANES * (c + 1)] for c in range(2)] for g in range(3)
    ]
    lane = lax.broadcasted_iota(i32, (1, LANES), 1)
    row8 = lax.broadcasted_iota(i32, (8, LANES), 0)

    @pl.loop(0, tiles, unroll=8)
    def _(tile):
        owner = owners[tile]
        rank = seen[owner]
        seen[owner] = rank + 1
        slot = owner * PER_OWNER + rank
        slots[tile] = slot
        base = slot * SLOT_ROWS
        ids = jnp.broadcast_to(cam_ids[pl.ds(tile, 1), :], (8, LANES))
        low = ids & (LANES - 1)
        upper = ids >= LANES
        picked = [
            jnp.where(upper, lookup(tables[g][1], low), lookup(tables[g][0], low)) for g in range(3)
        ]
        first = cam_jac[tile, 0:8, :] * picked[0]
        second = cam_jac[tile, 8:16, :] * picked[1]
        third = cam_jac[tile, 16:18, :] * picked[2][0:2]
        valid = lane < counts[tile]
        err0 = jnp.sum(first + jnp.where(row8 < 1, second, 0.0), axis=0, keepdims=True)
        err1 = jnp.sum(jnp.where(row8 < 1, 0.0, second), axis=0, keepdims=True) + jnp.sum(
            third, axis=0, keepdims=True
        )
        payload[pl.ds(base, 6), :] = jnp.where(valid, pt_jac[tile], 0.0)
        payload[pl.ds(base + 6, 1), :] = jnp.where(valid, err0, 0.0)
        payload[pl.ds(base + 7, 1), :] = jnp.where(valid, err1, 0.0)
        payload[pl.ds(base + 8, 1), :] = point_ids[pl.ds(tile, 1), :].astype(f32)


def solve_points(rhs, normal, damping):
    upper_aa = normal[0] + damping
    upper_ab = normal[1]
    upper_ac = normal[2]
    upper_bb = normal[3] + damping
    upper_bc = normal[4]
    upper_cc = normal[5] + damping
    minor_aa = upper_bb * upper_cc - upper_bc * upper_bc
    minor_ab = upper_ac * upper_bc - upper_ab * upper_cc
    minor_ac = upper_ab * upper_bc - upper_ac * upper_bb
    minor_bb = upper_aa * upper_cc - upper_ac * upper_ac
    minor_bc = upper_ab * upper_ac - upper_aa * upper_bc
    minor_cc = upper_aa * upper_bb - upper_ab * upper_ab
    determ = upper_aa * minor_aa + upper_ab * minor_ab + upper_ac * minor_ac
    return (
        (minor_aa * rhs[0] + minor_ab * rhs[1] + minor_ac * rhs[2]) / determ,
        (minor_ab * rhs[0] + minor_bb * rhs[1] + minor_bc * rhs[2]) / determ,
        (minor_ac * rhs[0] + minor_bc * rhs[1] + minor_cc * rhs[2]) / determ,
    )


def point_kernel(received, damping, remain, terms, left, right, sums, answers):
    slots = remain.shape[0] // 2
    groups = slots // GROUP
    uppers = damping.shape[0]
    rows = GROUP * SLOT_ROWS
    terms[...] = jnp.zeros(terms.shape, f32)
    sums[...] = jnp.zeros(sums.shape, f32)
    low_of_row = lax.broadcasted_iota(i32, (POINT_LOW, LANES), 0).astype(bf16)

    @pl.loop(0, groups)
    def _(group):
        base = group * rows
        jac = [received[pl.ds(base + r, GROUP, stride=SLOT_ROWS), :] for r in range(6)]
        err0 = received[pl.ds(base + 6, GROUP, stride=SLOT_ROWS), :]
        err1 = received[pl.ds(base + 7, GROUP, stride=SLOT_ROWS), :]
        ids = received[pl.ds(base + 8, GROUP, stride=SLOT_ROWS), :].astype(i32)
        upper = (ids // POINT_LOW).astype(f32)
        lower = (ids & (POINT_LOW - 1)).astype(f32)
        values = [jac[a] * err0 + jac[3 + a] * err1 for a in range(3)]
        for a, b in ((0, 0), (0, 1), (0, 2), (1, 1), (1, 2), (2, 2)):
            values.append(jac[a] * jac[b] + jac[3 + a] * jac[3 + b])
        for term, value in enumerate(values):
            for part, piece in enumerate(split(value)):
                terms[pl.ds(part * 9 + term, GROUP, stride=TERM_ROWS), :] = piece
        for s in range(GROUP):
            columns = slice(s * LANES, (s + 1) * LANES)
            block = terms[s * TERM_ROWS : (s + 1) * TERM_ROWS, :].astype(bf16)
            upper_row = jnp.broadcast_to(upper[s : s + 1, :], (TERM_ROWS, LANES)).astype(bf16)
            lower_row = jnp.broadcast_to(lower[s : s + 1, :], (POINT_LOW, LANES)).astype(bf16)
            for h in range(uppers):
                left[h * TERM_ROWS : (h + 1) * TERM_ROWS, columns] = jnp.where(
                    upper_row == jnp.asarray(h, bf16), block, jnp.zeros_like(block)
                )
            right[:, columns] = jnp.where(
                low_of_row == lower_row, jnp.ones((), bf16), jnp.zeros((), bf16)
            )
        added = contract(left[...], right[...])
        for half in range(2):
            sums[half] += added[:, half * LANES : (half + 1) * LANES]

    for half in range(2):
        columns = slice(half * LANES, (half + 1) * LANES)
        total = []
        for term in range(9):
            pieces = [
                sums[half, pl.ds(part * 9 + term, uppers, stride=TERM_ROWS), :]
                for part in range(PARTS)
            ]
            total.append(pieces[0] + (pieces[1] + pieces[2]))
        solved = solve_points(total[:3], total[3:], damping[:, columns])
        for a in range(3):
            answers[pl.ds((a * 2 + half) * uppers, uppers), :] = solved[a]

    @pl.loop(0, groups)
    def _(group):
        base = group * rows
        ids = received[pl.ds(base + 8, GROUP, stride=SLOT_ROWS), :].astype(i32)
        lane = ids & (LANES - 1)
        chunk = ids // LANES
        got = [None] * 3
        for k in range(2 * uppers):
            h, half = k // 2, k % 2
            for a in range(3):
                row = (a * 2 + half) * uppers + h
                table = jnp.broadcast_to(answers[row : row + 1, :], (GROUP, LANES))
                value = lookup(table, lane)
                got[a] = value if k == 0 else jnp.where(chunk == k, value, got[a])
        for r in range(2):
            image = sum(
                received[pl.ds(base + 3 * r + a, GROUP, stride=SLOT_ROWS), :] * got[a]
                for a in range(3)
            )
            error = received[pl.ds(base + 6 + r, GROUP, stride=SLOT_ROWS), :]
            remain[pl.ds(group * 2 * GROUP + r, GROUP, stride=2), :] = error - image


def camera_kernel(slots, remain, cam_jac, cam_ids, image, pieces, left, right):
    tiles = cam_ids.shape[0]
    cams = right.shape[0]
    copies = image.shape[0] // 18
    row = lax.broadcasted_iota(i32, (18, LANES), 0)
    cam_of_row = lax.broadcasted_iota(i32, (cams, LANES), 0).astype(bf16)
    pieces[...] = jnp.zeros(pieces.shape, f32)

    def step(group, total):
        for s in range(GROUP):
            tile = group * GROUP + s
            columns = slice(s * LANES, (s + 1) * LANES)
            base = slots[tile] * 2
            value = cam_jac[tile] * jnp.where(
                row < 9, remain[pl.ds(base, 1), :], remain[pl.ds(base + 1, 1), :]
            )
            pieces[s * TERM_ROWS : s * TERM_ROWS + 18, :] = value
            block = pieces[s * TERM_ROWS : (s + 1) * TERM_ROWS, :]
            for part, piece in enumerate(split(block)):
                left[part * TERM_ROWS : (part + 1) * TERM_ROWS, columns] = piece.astype(bf16)
            ids = jnp.broadcast_to(cam_ids[pl.ds(tile, 1), :], (cams, LANES)).astype(f32)
            right[:, columns] = jnp.where(
                cam_of_row == ids.astype(bf16), jnp.ones((), bf16), jnp.zeros((), bf16)
            )
        return total + contract(left[...], right[...])

    total = lax.fori_loop(
        0, tiles // GROUP, step, jnp.zeros((PARTS * TERM_ROWS, cams), f32)
    )
    merged = total[0:32] + (total[32:64] + total[64:96])
    for half in range(2):
        pieces[0:32, :] = merged[:, half * LANES : (half + 1) * LANES]
        summed = pieces[0:9, :] + pieces[9:18, :]
        for copy in range(copies):
            image[copy * 18 + half * 9 : copy * 18 + half * 9 + 9, :] = summed


def apply_blocks(precond, vector):
    total = None
    for j in range(9):
        term = precond[9 * j : 9 * j + 9, :] * vector[j : j + 1, :]
        total = term if total is None else total + term
    return total


def scalar_kernel(received, residual, direction, damping, precond, image, first_z, slope, scalars):
    copies = received.shape[0] // 18
    for half in range(2):
        columns = slice(half * LANES, (half + 1) * LANES)
        total = received[half * 9 : half * 9 + 9, :]
        for copy in range(1, copies):
            total = total + received[copy * 18 + half * 9 : copy * 18 + half * 9 + 9, :]
        image[:, columns] = damping[:, columns] * direction[:, columns] + total
    z = apply_blocks(precond, residual)
    y = apply_blocks(precond, image)
    first_z[...] = z
    slope[...] = y
    res = residual[...]
    img = image[...]
    sums = [
        jnp.sum(res * z),
        jnp.sum(direction[...] * img),
        jnp.sum(img * z + res * y),
        jnp.sum(img * y),
    ]
    lane = lax.broadcasted_iota(i32, scalars.shape, 1)
    row = jnp.zeros(scalars.shape, f32)
    for k, value in enumerate(sums):
        row = jnp.where(lane == k, value, row)
    scalars[...] = row


def final_kernel(
    scalars,
    solution_in,
    residual,
    direction,
    image,
    first_z,
    slope,
    new_solution,
    new_residual,
    new_direction,
):
    total = jnp.sum(scalars[...], axis=0, keepdims=True)
    lane = lax.broadcasted_iota(i32, total.shape, 1)
    rz, pq, cross, square = [
        jnp.sum(jnp.where(lane == k, total, 0.0), axis=1, keepdims=True) for k in range(4)
    ]
    alpha = rz / pq
    rz1 = rz + alpha * (alpha * square - cross)
    way = direction[...]
    new_solution[...] = solution_in[...] + alpha * way
    new_residual[...] = residual[...] - alpha * image[...]
    new_direction[...] = first_z[...] - alpha * slope[...] + (rz1 / rz) * way


SMEM = pl.BlockSpec(memory_space=pltpu.SMEM)
VMEM = pl.BlockSpec(memory_space=pltpu.VMEM)
LIMIT = pltpu.CompilerParams(vmem_limit_bytes=32 * 1024 * 1024)


def shape(*dims, dtype=f32):
    return jax.ShapeDtypeStruct(dims, dtype)


def pack(owners, counts, direction, cam_ids, cam_jac, pt_jac, point_ids, owner_count):
    tiles = cam_ids.shape[0]
    return pl.pallas_call(
        pack_kernel,
        out_shape=(
            shape(owner_count * PER_OWNER * SLOT_ROWS, LANES),
            shape(tiles, dtype=i32),
        ),
        in_specs=[SMEM, SMEM] + [VMEM] * 5,
        out_specs=(VMEM, SMEM),
        scratch_shapes=[
            pltpu.SMEM((owner_count,), i32),
            pltpu.VMEM((24, direction.shape[1]), f32),
        ],
        compiler_params=LIMIT,
        name="pack_tiles",
    )(owners, counts, direction, cam_ids, cam_jac, pt_jac, point_ids)


def points(received, damping):
    slots = received.shape[0] // SLOT_ROWS
    uppers = damping.shape[0]
    return pl.pallas_call(
        point_kernel,
        out_shape=shape(slots * 2, LANES),
        in_specs=[VMEM] * 2,
        out_specs=VMEM,
        scratch_shapes=[
            pltpu.VMEM((GROUP * TERM_ROWS, LANES), f32),
            pltpu.VMEM((uppers * TERM_ROWS, GROUP * LANES), bf16),
            pltpu.VMEM((POINT_LOW, GROUP * LANES), bf16),
            pltpu.VMEM((2, uppers * TERM_ROWS, LANES), f32),
            pltpu.VMEM((6 * uppers, LANES), f32),
        ],
        compiler_params=LIMIT,
        name="solve_points",
    )(received, damping)


def cameras(slots, remain, cam_jac, cam_ids, cams, copies):
    return pl.pallas_call(
        camera_kernel,
        out_shape=shape(copies * 18, LANES),
        in_specs=[SMEM] + [VMEM] * 3,
        out_specs=VMEM,
        scratch_shapes=[
            pltpu.VMEM((GROUP * TERM_ROWS, LANES), f32),
            pltpu.VMEM((PARTS * TERM_ROWS, GROUP * LANES), bf16),
            pltpu.VMEM((cams, GROUP * LANES), bf16),
        ],
        compiler_params=LIMIT,
        name="sum_cameras",
    )(slots, remain, cam_jac, cam_ids)


def scalar_sums(received, residual, direction, damping, precond, owner_count):
    vector = shape(*residual.shape)
    return pl.pallas_call(
        scalar_kernel,
        out_shape=(vector, vector, vector, shape(owner_count, LANES)),
        in_specs=[VMEM] * 5,
        out_specs=(VMEM,) * 4,
        compiler_params=LIMIT,
        name="camera_scalars",
    )(received, residual, direction, damping, precond)


def finish(scalars, solution_in, residual, direction, image, first_z, slope):
    vector = shape(*residual.shape)
    return pl.pallas_call(
        final_kernel,
        out_shape=(vector,) * 3,
        in_specs=[VMEM] * 7,
        out_specs=(VMEM,) * 3,
        compiler_params=LIMIT,
        name="update_vectors",
    )(scalars, solution_in, residual, direction, image, first_z, slope)


def exchange(rows, axis, count):
    depth = rows.shape[0] // count
    sent = rows.reshape(count, depth, 1, LANES)
    got = lax.all_to_all(sent, axis, split_axis=0, concat_axis=0, tiled=True)
    return got.reshape(count * depth, LANES)


def body(
    solution,
    residual,
    direction,
    cam_damping,
    precond,
    pt_damping,
    cam_jac,
    pt_jac,
    cam_ids,
    point_ids,
    owners,
    valid_counts,
):
    owner_count = lax.axis_size("cam")
    copies = lax.axis_size("pt")
    payload, slots = pack(
        owners.reshape(-1),
        valid_counts,
        direction,
        cam_ids,
        cam_jac,
        pt_jac,
        point_ids,
        owner_count,
    )
    received = exchange(payload, "cam", owner_count)
    remain = points(received, pt_damping.reshape(-1, POINT_LOW))
    returned = exchange(remain, "cam", owner_count)
    image_rows = cameras(slots, returned, cam_jac, cam_ids, direction.shape[1], copies)
    image_all = exchange(image_rows, "pt", copies)
    image, first_z, slope, scalars = scalar_sums(
        image_all, residual, direction, cam_damping, precond, owner_count
    )
    scalars_all = exchange(scalars, "cam", owner_count)
    return finish(scalars_all, solution, residual, direction, image, first_z, slope)


def solution(mesh):
    return jax.shard_map(
        body,
        mesh=mesh,
        in_specs=(
            P(None, "cam"),
            P(None, "cam"),
            P(None, "cam"),
            P(None, "cam"),
            P(None, "cam"),
            P(("cam", "pt")),
            P(("cam", "pt"), None, None),
            P(("cam", "pt"), None, None),
            P(("cam", "pt"), None),
            P(("cam", "pt"), None),
            P(("cam", "pt"), None),
            P(("cam", "pt")),
        ),
        out_specs=(P(None, "cam"), P(None, "cam"), P(None, "cam")),
        check_vma=False,
    )
```

```python
import functools

import jax
import jax.numpy as jnp
from jax import lax
from jax.experimental import pallas as pl
from jax.experimental.pallas import tpu as pltpu
from jax.sharding import PartitionSpec as P

LANES = 128
PER_OWNER = 2
SLOT_ROWS = 9
TERM_ROWS = 32
GROUP = 8
POINT_LOW = 256
PARTS = 3
CHUNK = 2
PLACES = 2

f32 = jnp.float32
bf16 = jnp.bfloat16
i32 = jnp.int32


def split(value):
    high = value.astype(bf16).astype(f32)
    rest = value - high
    middle = rest.astype(bf16).astype(f32)
    low = (rest - middle).astype(bf16).astype(f32)
    return high, middle, low


def lookup(table, index):
    return jnp.take_along_axis(table, index, axis=1, mode="promise_in_bounds")


def contract(left, right):
    return lax.dot_general(left, right, (((1,), (1,)), ((), ())), preferred_element_type=f32)


def store_terms(terms, values, group):
    base = group * GROUP * TERM_ROWS
    for term, value in enumerate(values):
        for part, piece in enumerate(split(value)):
            terms[pl.ds(base + part * 9 + term, GROUP, stride=TERM_ROWS), :] = piece


def one_hot(row_index, ids):
    return jnp.where(row_index == ids, jnp.ones((), bf16), jnp.zeros((), bf16))


def spread(value, s, rows):
    return jnp.broadcast_to(value[s : s + 1, :], (rows, LANES)).astype(bf16)


def pack_kernel(
    owners, counts, direction, cam_ids, cam_jac, pt_jac, point_ids, payload, slots, seen, stage
):
    tiles = cam_ids.shape[0]
    payload[...] = jnp.zeros(payload.shape, f32)
    for index in range(seen.shape[0]):
        seen[index] = 0
    lane = lax.broadcasted_iota(i32, (GROUP, LANES), 1)
    row = lax.broadcasted_iota(i32, (GROUP, LANES), 0)
    for group in range(tiles // GROUP):
        span = slice(group * GROUP, (group + 1) * GROUP)
        ids = cam_ids[span, :]
        low = ids & (LANES - 1)
        upper = ids >= LANES
        errors = [None, None]
        for j in range(9):
            tables = [
                jnp.broadcast_to(direction[j : j + 1, LANES * c : LANES * (c + 1)], (GROUP, LANES))
                for c in range(2)
            ]
            picked = jnp.where(upper, lookup(tables[1], low), lookup(tables[0], low))
            for r in range(2):
                term = cam_jac[9 * r + j, span, :] * picked
                errors[r] = term if errors[r] is None else errors[r] + term
        used = jnp.zeros((GROUP, LANES), i32)
        for s in range(GROUP):
            used = jnp.where(row == s, counts[group * GROUP + s], used)
        valid = lane < used
        values = [pt_jac[a, span, :] for a in range(6)] + errors
        for r, value in enumerate(values):
            stage[pl.ds(group * GROUP * SLOT_ROWS + r, GROUP, stride=SLOT_ROWS), :] = jnp.where(
                valid, value, 0.0
            )
        stage[pl.ds(group * GROUP * SLOT_ROWS + 8, GROUP, stride=SLOT_ROWS), :] = point_ids[
            span, :
        ].astype(f32)
    for tile in range(tiles):
        owner = owners[tile]
        rank = seen[owner]
        seen[owner] = rank + 1
        slot = owner * PER_OWNER + rank
        slots[tile] = slot
        payload[pl.ds(slot * SLOT_ROWS, SLOT_ROWS), :] = stage[
            tile * SLOT_ROWS : (tile + 1) * SLOT_ROWS, :
        ]


def solve_points(rhs, normal, damping):
    upper_aa = normal[0] + damping
    upper_ab = normal[1]
    upper_ac = normal[2]
    upper_bb = normal[3] + damping
    upper_bc = normal[4]
    upper_cc = normal[5] + damping
    minor_aa = upper_bb * upper_cc - upper_bc * upper_bc
    minor_ab = upper_ac * upper_bc - upper_ab * upper_cc
    minor_ac = upper_ab * upper_bc - upper_ac * upper_bb
    minor_bb = upper_aa * upper_cc - upper_ac * upper_ac
    minor_bc = upper_ab * upper_ac - upper_aa * upper_bc
    minor_cc = upper_aa * upper_bb - upper_ab * upper_ab
    determ = upper_aa * minor_aa + upper_ab * minor_ab + upper_ac * minor_ac
    return (
        (minor_aa * rhs[0] + minor_ab * rhs[1] + minor_ac * rhs[2]) / determ,
        (minor_ab * rhs[0] + minor_bb * rhs[1] + minor_bc * rhs[2]) / determ,
        (minor_ac * rhs[0] + minor_bc * rhs[1] + minor_cc * rhs[2]) / determ,
    )


def point_kernel(received, damping, remain, terms, sums, answers):
    slots = remain.shape[0] // 2
    groups = slots // GROUP
    uppers = damping.shape[0]
    rows = GROUP * SLOT_ROWS
    terms[...] = jnp.zeros(terms.shape, f32)
    sums[...] = jnp.zeros(sums.shape, f32)
    low_of_row = lax.broadcasted_iota(i32, (POINT_LOW, LANES), 0).astype(bf16)

    def chunk(start, place):
        lefts, rights = [], []
        for k in range(CHUNK):
            base = (start + k) * rows
            jac = [received[pl.ds(base + r, GROUP, stride=SLOT_ROWS), :] for r in range(6)]
            err0 = received[pl.ds(base + 6, GROUP, stride=SLOT_ROWS), :]
            err1 = received[pl.ds(base + 7, GROUP, stride=SLOT_ROWS), :]
            ids = received[pl.ds(base + 8, GROUP, stride=SLOT_ROWS), :].astype(i32)
            upper = (ids // POINT_LOW).astype(f32)
            lower = (ids & (POINT_LOW - 1)).astype(f32)
            values = [jac[a] * err0 + jac[3 + a] * err1 for a in range(3)]
            for a, b in ((0, 0), (0, 1), (0, 2), (1, 1), (1, 2), (2, 2)):
                values.append(jac[a] * jac[b] + jac[3 + a] * jac[3 + b])
            store_terms(terms, values, place * CHUNK + k)
            for s in range(GROUP):
                at = ((place * CHUNK + k) * GROUP + s) * TERM_ROWS
                block = terms[at : at + TERM_ROWS, :].astype(bf16)
                upper_row = spread(upper, s, TERM_ROWS)
                lefts.append(
                    jnp.concatenate(
                        [
                            jnp.where(upper_row == jnp.asarray(h, bf16), block, jnp.zeros_like(block))
                            for h in range(uppers)
                        ],
                        axis=0,
                    )
                )
                rights.append(one_hot(low_of_row, spread(lower, s, POINT_LOW)))
        return contract(jnp.concatenate(lefts, axis=1), jnp.concatenate(rights, axis=1))

    @pl.loop(0, groups // (CHUNK * PLACES))
    def _(step):
        for place in range(PLACES):
            added = chunk((step * PLACES + place) * CHUNK, place)
            for half in range(2):
                sums[half] += added[:, half * LANES : (half + 1) * LANES]

    for half in range(2):
        columns = slice(half * LANES, (half + 1) * LANES)
        total = []
        for term in range(9):
            pieces = [
                sums[half, pl.ds(part * 9 + term, uppers, stride=TERM_ROWS), :]
                for part in range(PARTS)
            ]
            total.append(pieces[0] + (pieces[1] + pieces[2]))
        solved = solve_points(total[:3], total[3:], damping[:, columns])
        for a in range(3):
            answers[pl.ds((a * 2 + half) * uppers, uppers), :] = solved[a]

    @pl.loop(0, groups)
    def _(group):
        base = group * rows
        ids = received[pl.ds(base + 8, GROUP, stride=SLOT_ROWS), :].astype(i32)
        lane = ids & (LANES - 1)
        chunk = ids // LANES
        got = [None] * 3
        for k in range(2 * uppers):
            h, half = k // 2, k % 2
            for a in range(3):
                row = (a * 2 + half) * uppers + h
                table = jnp.broadcast_to(answers[row : row + 1, :], (GROUP, LANES))
                value = lookup(table, lane)
                got[a] = value if k == 0 else jnp.where(chunk == k, value, got[a])
        for r in range(2):
            image = sum(
                received[pl.ds(base + 3 * r + a, GROUP, stride=SLOT_ROWS), :] * got[a]
                for a in range(3)
            )
            error = received[pl.ds(base + 6 + r, GROUP, stride=SLOT_ROWS), :]
            remain[pl.ds(group * 2 * GROUP + r, GROUP, stride=2), :] = error - image


def camera_kernel(slots, remain, cam_jac, cam_ids, image, terms, stage):
    tiles = cam_ids.shape[0]
    cams = 2 * LANES
    copies = image.shape[0] // 18
    cam_of_row = lax.broadcasted_iota(i32, (cams, LANES), 0).astype(bf16)
    terms[...] = jnp.zeros(terms.shape, f32)
    for tile in range(tiles):
        stage[2 * tile : 2 * tile + 2, :] = remain[pl.ds(slots[tile] * 2, 2), :]
    total = None
    for start in range(0, tiles // GROUP, CHUNK):
        lefts, rights = [], []
        for group in range(start, start + CHUNK):
            span = slice(group * GROUP, (group + 1) * GROUP)
            rest = [stage[pl.ds(2 * group * GROUP + r, GROUP, stride=2), :] for r in range(2)]
            values = [
                cam_jac[j, span, :] * rest[0] + cam_jac[9 + j, span, :] * rest[1] for j in range(9)
            ]
            store_terms(terms, values, group)
            ids = cam_ids[span, :].astype(f32)
            for s in range(GROUP):
                at = (group * GROUP + s) * TERM_ROWS
                lefts.append(terms[at : at + TERM_ROWS, :].astype(bf16))
                rights.append(one_hot(cam_of_row, spread(ids, s, cams)))
        added = contract(jnp.concatenate(lefts, axis=1), jnp.concatenate(rights, axis=1))
        total = added if total is None else total + added
    for half in range(2):
        terms[0:TERM_ROWS, :] = total[:, half * LANES : (half + 1) * LANES]
        summed = terms[0:9, :] + (terms[9:18, :] + terms[18:27, :])
        for copy in range(copies):
            image[copy * 18 + half * 9 : copy * 18 + half * 9 + 9, :] = summed


def apply_blocks(precond, vector):
    total = None
    for j in range(9):
        term = precond[9 * j : 9 * j + 9, :] * vector[j : j + 1, :]
        total = term if total is None else total + term
    return total


def scalar_kernel(received, residual, direction, damping, precond, image, first_z, slope, scalars):
    copies = received.shape[0] // 18
    for half in range(2):
        columns = slice(half * LANES, (half + 1) * LANES)
        total = received[half * 9 : half * 9 + 9, :]
        for copy in range(1, copies):
            total = total + received[copy * 18 + half * 9 : copy * 18 + half * 9 + 9, :]
        image[:, columns] = damping[:, columns] * direction[:, columns] + total
    z = apply_blocks(precond, residual)
    y = apply_blocks(precond, image)
    first_z[...] = z
    slope[...] = y
    res = residual[...]
    img = image[...]
    sums = [
        jnp.sum(res * z),
        jnp.sum(direction[...] * img),
        jnp.sum(img * z + res * y),
        jnp.sum(img * y),
    ]
    lane = lax.broadcasted_iota(i32, scalars.shape, 1)
    row = jnp.zeros(scalars.shape, f32)
    for k, value in enumerate(sums):
        row = jnp.where(lane == k, value, row)
    scalars[...] = row


def final_kernel(
    scalars,
    solution_in,
    residual,
    direction,
    image,
    first_z,
    slope,
    new_solution,
    new_residual,
    new_direction,
):
    total = jnp.sum(scalars[...], axis=0, keepdims=True)
    lane = lax.broadcasted_iota(i32, total.shape, 1)
    rz, pq, cross, square = [
        jnp.sum(jnp.where(lane == k, total, 0.0), axis=1, keepdims=True) for k in range(4)
    ]
    alpha = rz / pq
    rz1 = rz + alpha * (alpha * square - cross)
    way = direction[...]
    new_solution[...] = solution_in[...] + alpha * way
    new_residual[...] = residual[...] - alpha * image[...]
    new_direction[...] = first_z[...] - alpha * slope[...] + (rz1 / rz) * way


SMEM = pl.BlockSpec(memory_space=pltpu.SMEM)
VMEM = pl.BlockSpec(memory_space=pltpu.VMEM)
LIMIT = pltpu.CompilerParams(vmem_limit_bytes=32 * 1024 * 1024)


def shape(*dims, dtype=f32):
    return jax.ShapeDtypeStruct(dims, dtype)


def pack(owners, counts, direction, cam_ids, cam_jac, pt_jac, point_ids, owner_count):
    tiles = cam_ids.shape[0]
    return pl.pallas_call(
        pack_kernel,
        out_shape=(
            shape(owner_count * PER_OWNER * SLOT_ROWS, LANES),
            shape(tiles, dtype=i32),
        ),
        in_specs=[SMEM, SMEM] + [VMEM] * 5,
        out_specs=(VMEM, SMEM),
        scratch_shapes=[
            pltpu.SMEM((owner_count,), i32),
            pltpu.VMEM((tiles * SLOT_ROWS, LANES), f32),
        ],
        compiler_params=LIMIT,
        name="pack_tiles",
    )(owners, counts, direction, cam_ids, cam_jac, pt_jac, point_ids)


def points(received, damping):
    slots = received.shape[0] // SLOT_ROWS
    uppers = damping.shape[0]
    return pl.pallas_call(
        point_kernel,
        out_shape=shape(slots * 2, LANES),
        in_specs=[VMEM] * 2,
        out_specs=VMEM,
        scratch_shapes=[
            pltpu.VMEM((PLACES * CHUNK * GROUP * TERM_ROWS, LANES), f32),
            pltpu.VMEM((2, uppers * TERM_ROWS, LANES), f32),
            pltpu.VMEM((6 * uppers, LANES), f32),
        ],
        compiler_params=LIMIT,
        name="solve_points",
    )(received, damping)


def cameras(slots, remain, cam_jac, cam_ids, copies):
    tiles = cam_ids.shape[0]
    return pl.pallas_call(
        camera_kernel,
        out_shape=shape(copies * 18, LANES),
        in_specs=[SMEM] + [VMEM] * 3,
        out_specs=VMEM,
        scratch_shapes=[
            pltpu.VMEM((tiles * TERM_ROWS, LANES), f32),
            pltpu.VMEM((2 * tiles, LANES), f32),
        ],
        compiler_params=LIMIT,
        name="sum_cameras",
    )(slots, remain, cam_jac, cam_ids)


def scalar_sums(received, residual, direction, damping, precond, owner_count):
    vector = shape(*residual.shape)
    return pl.pallas_call(
        scalar_kernel,
        out_shape=(vector, vector, vector, shape(owner_count, LANES)),
        in_specs=[VMEM] * 5,
        out_specs=(VMEM,) * 4,
        compiler_params=LIMIT,
        name="camera_scalars",
    )(received, residual, direction, damping, precond)


def finish(scalars, solution_in, residual, direction, image, first_z, slope):
    vector = shape(*residual.shape)
    return pl.pallas_call(
        final_kernel,
        out_shape=(vector,) * 3,
        in_specs=[VMEM] * 7,
        out_specs=(VMEM,) * 3,
        compiler_params=LIMIT,
        name="update_vectors",
    )(scalars, solution_in, residual, direction, image, first_z, slope)


def exchange(rows, axis, count):
    depth = rows.shape[0] // count
    sent = rows.reshape(count, depth, 1, LANES)
    got = lax.all_to_all(sent, axis, split_axis=0, concat_axis=0, tiled=True)
    return got.reshape(count * depth, LANES)


def body(
    solution,
    residual,
    direction,
    cam_damping,
    precond,
    pt_damping,
    cam_jac,
    pt_jac,
    cam_ids,
    point_ids,
    owners,
    valid_counts,
):
    owner_count = lax.axis_size("cam")
    copies = lax.axis_size("pt")
    cam_jac = cam_jac.transpose(1, 0, 2)
    pt_jac = pt_jac.transpose(1, 0, 2)
    payload, slots = pack(
        owners.reshape(-1),
        valid_counts,
        direction,
        cam_ids,
        cam_jac,
        pt_jac,
        point_ids,
        owner_count,
    )
    received = exchange(payload, "cam", owner_count)
    remain = points(received, pt_damping.reshape(-1, POINT_LOW))
    returned = exchange(remain, "cam", owner_count)
    image_rows = cameras(slots, returned, cam_jac, cam_ids, copies)
    image_all = exchange(image_rows, "pt", copies)
    image, first_z, slope, scalars = scalar_sums(
        image_all, residual, direction, cam_damping, precond, owner_count
    )
    scalars_all = exchange(scalars, "cam", owner_count)
    return finish(scalars_all, solution, residual, direction, image, first_z, slope)


def solution(mesh):
    return jax.shard_map(
        body,
        mesh=mesh,
        in_specs=(
            P(None, "cam"),
            P(None, "cam"),
            P(None, "cam"),
            P(None, "cam"),
            P(None, "cam"),
            P(("cam", "pt")),
            P(("cam", "pt"), None, None),
            P(("cam", "pt"), None, None),
            P(("cam", "pt"), None),
            P(("cam", "pt"), None),
            P(("cam", "pt"), None),
            P(("cam", "pt")),
        ),
        out_specs=(P(None, "cam"), P(None, "cam"), P(None, "cam")),
        check_vma=False,
    )
```

```python
import functools

import jax
import jax.numpy as jnp
from jax import lax
from jax.experimental import pallas as pl
from jax.experimental.pallas import tpu as pltpu
from jax.sharding import PartitionSpec as P

LANES = 128
PER_OWNER = 2
SLOT_ROWS = 9
TERM_ROWS = 32
GROUP = 8
POINT_LOW = 256
PARTS = 3
CHUNK = 2
PLACES = 4
WIDE = 2
CAM_CHUNK = 4

f32 = jnp.float32
bf16 = jnp.bfloat16
i32 = jnp.int32


def split(value):
    high = value.astype(bf16).astype(f32)
    rest = value - high
    middle = rest.astype(bf16).astype(f32)
    low = (rest - middle).astype(bf16).astype(f32)
    return high, middle, low


def lookup(table, index):
    return jnp.take_along_axis(table, index, axis=1, mode="promise_in_bounds")


def contract(left, right):
    return lax.dot_general(left, right, (((1,), (1,)), ((), ())), preferred_element_type=f32)


def store_terms(terms, values, group):
    base = group * GROUP * TERM_ROWS
    for term, value in enumerate(values):
        for part, piece in enumerate(split(value)):
            terms[pl.ds(base + part * 9 + term, GROUP, stride=TERM_ROWS), :] = piece


def one_hot(row_index, ids):
    return jnp.where(row_index == ids, jnp.ones((), bf16), jnp.zeros((), bf16))


def spread(value, s, rows):
    return jnp.broadcast_to(value[s : s + 1, :], (rows, LANES)).astype(bf16)


def pack_kernel(*refs):
    sources, (payload, places, seen, stage), held, sem = refs[:7], refs[7:11], refs[11:18], refs[18]
    copies = [
        pltpu.make_async_copy(source, target, sem.at[k])
        for k, (source, target) in enumerate(zip(sources, held))
    ]
    for copy in copies:
        copy.start()
    payload[...] = jnp.zeros(payload.shape, f32)
    owners, counts, direction, cam_ids, cam_jac, pt_jac, point_ids = held
    tiles = cam_ids.shape[0]
    for index in range(seen.shape[0]):
        seen[index] = 0
    for copy in copies:
        copy.wait()
    lane = lax.broadcasted_iota(i32, (GROUP, LANES), 1)
    row = lax.broadcasted_iota(i32, (GROUP, LANES), 0)
    for group in range(tiles // GROUP):
        span = slice(group * GROUP, (group + 1) * GROUP)
        ids = cam_ids[span, :]
        low = ids & (LANES - 1)
        upper = ids >= LANES
        errors = [None, None]
        for j in range(9):
            tables = [
                jnp.broadcast_to(direction[j : j + 1, LANES * c : LANES * (c + 1)], (GROUP, LANES))
                for c in range(2)
            ]
            picked = jnp.where(upper, lookup(tables[1], low), lookup(tables[0], low))
            for r in range(2):
                term = cam_jac[9 * r + j, span, :] * picked
                errors[r] = term if errors[r] is None else errors[r] + term
        used = jnp.zeros((GROUP, LANES), i32)
        for s in range(GROUP):
            used = jnp.where(row == s, counts[group * GROUP + s], used)
        valid = lane < used
        values = [pt_jac[a, span, :] for a in range(6)] + errors
        for r, value in enumerate(values):
            stage[pl.ds(group * GROUP * SLOT_ROWS + r, GROUP, stride=SLOT_ROWS), :] = jnp.where(
                valid, value, 0.0
            )
        stage[pl.ds(group * GROUP * SLOT_ROWS + 8, GROUP, stride=SLOT_ROWS), :] = point_ids[
            span, :
        ].astype(f32)
    slot_lane = lax.broadcasted_iota(i32, (1, places.shape[1]), 1)
    for tile in range(tiles):
        owner = owners[tile]
        rank = seen[owner]
        seen[owner] = rank + 1
        slot = owner * PER_OWNER + rank
        places[tile : tile + 1, :] = jnp.where(slot_lane == slot, 1.0, 0.0)
        payload[pl.ds(slot * SLOT_ROWS, SLOT_ROWS), :] = stage[
            tile * SLOT_ROWS : (tile + 1) * SLOT_ROWS, :
        ]


def solve_points(rhs, normal, damping):
    upper_aa = normal[0] + damping
    upper_ab = normal[1]
    upper_ac = normal[2]
    upper_bb = normal[3] + damping
    upper_bc = normal[4]
    upper_cc = normal[5] + damping
    minor_aa = upper_bb * upper_cc - upper_bc * upper_bc
    minor_ab = upper_ac * upper_bc - upper_ab * upper_cc
    minor_ac = upper_ab * upper_bc - upper_ac * upper_bb
    minor_bb = upper_aa * upper_cc - upper_ac * upper_ac
    minor_bc = upper_ab * upper_ac - upper_aa * upper_bc
    minor_cc = upper_aa * upper_bb - upper_ab * upper_ab
    determ = upper_aa * minor_aa + upper_ab * minor_ab + upper_ac * minor_ac
    return (
        (minor_aa * rhs[0] + minor_ab * rhs[1] + minor_ac * rhs[2]) / determ,
        (minor_ab * rhs[0] + minor_bb * rhs[1] + minor_bc * rhs[2]) / determ,
        (minor_ac * rhs[0] + minor_bc * rhs[1] + minor_cc * rhs[2]) / determ,
    )


def point_kernel(received, damping, remain, terms, sums, answers):
    slots = remain.shape[0] // 2
    groups = slots // GROUP
    uppers = damping.shape[0]
    rows = GROUP * SLOT_ROWS
    terms[...] = jnp.zeros(terms.shape, f32)
    sums[...] = jnp.zeros(sums.shape, f32)
    low_of_row = lax.broadcasted_iota(i32, (POINT_LOW, LANES), 0).astype(bf16)

    def chunk(start, place):
        lefts, rights = [], []
        for k in range(CHUNK):
            base = (start + k) * rows
            jac = [received[pl.ds(base + r, GROUP, stride=SLOT_ROWS), :] for r in range(6)]
            err0 = received[pl.ds(base + 6, GROUP, stride=SLOT_ROWS), :]
            err1 = received[pl.ds(base + 7, GROUP, stride=SLOT_ROWS), :]
            ids = received[pl.ds(base + 8, GROUP, stride=SLOT_ROWS), :].astype(i32)
            upper = (ids // POINT_LOW).astype(f32)
            lower = (ids & (POINT_LOW - 1)).astype(f32)
            values = [jac[a] * err0 + jac[3 + a] * err1 for a in range(3)]
            for a, b in ((0, 0), (0, 1), (0, 2), (1, 1), (1, 2), (2, 2)):
                values.append(jac[a] * jac[b] + jac[3 + a] * jac[3 + b])
            store_terms(terms, values, place * CHUNK + k)
            for s in range(GROUP):
                at = ((place * CHUNK + k) * GROUP + s) * TERM_ROWS
                block = terms[at : at + TERM_ROWS, :].astype(bf16)
                upper_row = spread(upper, s, TERM_ROWS)
                lefts.append(
                    jnp.concatenate(
                        [
                            jnp.where(upper_row == jnp.asarray(h, bf16), block, jnp.zeros_like(block))
                            for h in range(uppers)
                        ],
                        axis=0,
                    )
                )
                rights.append(one_hot(low_of_row, spread(lower, s, POINT_LOW)))
        return contract(jnp.concatenate(lefts, axis=1), jnp.concatenate(rights, axis=1))

    @pl.loop(0, groups // (CHUNK * PLACES))
    def _(step):
        for place in range(PLACES):
            added = chunk((step * PLACES + place) * CHUNK, place)
            for half in range(2):
                sums[half] += added[:, half * LANES : (half + 1) * LANES]

    for half in range(2):
        columns = slice(half * LANES, (half + 1) * LANES)
        total = []
        for term in range(9):
            pieces = [
                sums[half, pl.ds(part * 9 + term, uppers, stride=TERM_ROWS), :]
                for part in range(PARTS)
            ]
            total.append(pieces[0] + (pieces[1] + pieces[2]))
        solved = solve_points(total[:3], total[3:], damping[:, columns])
        for a in range(3):
            answers[pl.ds((a * 2 + half) * uppers, uppers), :] = solved[a]

    @pl.loop(0, groups // WIDE)
    def _(step):
        bases = [(step * WIDE + w) * rows for w in range(WIDE)]
        ids = [
            received[pl.ds(base + 8, GROUP, stride=SLOT_ROWS), :].astype(i32) for base in bases
        ]
        lanes = [value & (LANES - 1) for value in ids]
        chunks = [value // LANES for value in ids]
        got = [[None] * 3 for _ in range(WIDE)]
        for k in range(2 * uppers):
            h, half = k // 2, k % 2
            for a in range(3):
                row = (a * 2 + half) * uppers + h
                table = jnp.broadcast_to(answers[row : row + 1, :], (GROUP, LANES))
                for w in range(WIDE):
                    value = lookup(table, lanes[w])
                    got[w][a] = value if k == 0 else jnp.where(chunks[w] == k, value, got[w][a])
        for w, base in enumerate(bases):
            for r in range(2):
                image = sum(
                    received[pl.ds(base + 3 * r + a, GROUP, stride=SLOT_ROWS), :] * got[w][a]
                    for a in range(3)
                )
                error = received[pl.ds(base + 6 + r, GROUP, stride=SLOT_ROWS), :]
                remain[pl.ds((step * WIDE + w) * 2 * GROUP + r, GROUP, stride=2), :] = error - image


def camera_kernel(places, remain, cam_jac, cam_ids, image, terms, stage):
    tiles = cam_ids.shape[0]
    cams = 2 * LANES
    copies = image.shape[0] // 18
    cam_of_row = lax.broadcasted_iota(i32, (cams, LANES), 0).astype(bf16)
    terms[...] = jnp.zeros(terms.shape, f32)
    chosen = places[...].astype(bf16)
    for r in range(2):
        high, middle, low = [
            lax.dot_general(
                chosen, piece.astype(bf16), (((1,), (0,)), ((), ())), preferred_element_type=f32
            )
            for piece in split(remain[pl.ds(r, places.shape[1], stride=2), :])
        ]
        stage[r] = high + (middle + low)
    total = None
    for start in range(0, tiles // GROUP, CAM_CHUNK):
        lefts, rights = [], []
        for group in range(start, start + CAM_CHUNK):
            span = slice(group * GROUP, (group + 1) * GROUP)
            rest = [stage[r, span, :] for r in range(2)]
            values = [
                cam_jac[j, span, :] * rest[0] + cam_jac[9 + j, span, :] * rest[1] for j in range(9)
            ]
            store_terms(terms, values, group)
            ids = cam_ids[span, :].astype(f32)
            for s in range(GROUP):
                at = (group * GROUP + s) * TERM_ROWS
                lefts.append(terms[at : at + TERM_ROWS, :].astype(bf16))
                rights.append(one_hot(cam_of_row, spread(ids, s, cams)))
        added = contract(jnp.concatenate(lefts, axis=1), jnp.concatenate(rights, axis=1))
        total = added if total is None else total + added
    for half in range(2):
        terms[0:TERM_ROWS, :] = total[:, half * LANES : (half + 1) * LANES]
        summed = terms[0:9, :] + (terms[9:18, :] + terms[18:27, :])
        for copy in range(copies):
            image[copy * 18 + half * 9 : copy * 18 + half * 9 + 9, :] = summed


def apply_blocks(precond, vector):
    total = None
    for j in range(9):
        term = precond[9 * j : 9 * j + 9, :] * vector[j : j + 1, :]
        total = term if total is None else total + term
    return total


def scalar_kernel(received, residual, direction, damping, precond, image, first_z, slope, scalars):
    copies = received.shape[0] // 18
    for half in range(2):
        columns = slice(half * LANES, (half + 1) * LANES)
        total = received[half * 9 : half * 9 + 9, :]
        for copy in range(1, copies):
            total = total + received[copy * 18 + half * 9 : copy * 18 + half * 9 + 9, :]
        image[:, columns] = damping[:, columns] * direction[:, columns] + total
    z = apply_blocks(precond, residual)
    y = apply_blocks(precond, image)
    first_z[...] = z
    slope[...] = y
    res = residual[...]
    img = image[...]
    sums = [
        jnp.sum(res * z),
        jnp.sum(direction[...] * img),
        jnp.sum(img * z + res * y),
        jnp.sum(img * y),
    ]
    lane = lax.broadcasted_iota(i32, scalars.shape, 1)
    row = jnp.zeros(scalars.shape, f32)
    for k, value in enumerate(sums):
        row = jnp.where(lane == k, value, row)
    scalars[...] = row


def final_kernel(
    scalars,
    solution_in,
    residual,
    direction,
    image,
    first_z,
    slope,
    new_solution,
    new_residual,
    new_direction,
):
    total = jnp.sum(scalars[...], axis=0, keepdims=True)
    lane = lax.broadcasted_iota(i32, total.shape, 1)
    rz, pq, cross, square = [
        jnp.sum(jnp.where(lane == k, total, 0.0), axis=1, keepdims=True) for k in range(4)
    ]
    alpha = rz / pq
    rz1 = rz + alpha * (alpha * square - cross)
    way = direction[...]
    new_solution[...] = solution_in[...] + alpha * way
    new_residual[...] = residual[...] - alpha * image[...]
    new_direction[...] = first_z[...] - alpha * slope[...] + (rz1 / rz) * way


SMEM = pl.BlockSpec(memory_space=pltpu.SMEM)
VMEM = pl.BlockSpec(memory_space=pltpu.VMEM)
LIMIT = pltpu.CompilerParams(vmem_limit_bytes=32 * 1024 * 1024)


def shape(*dims, dtype=f32):
    return jax.ShapeDtypeStruct(dims, dtype)


def pack(owners, counts, direction, cam_ids, cam_jac, pt_jac, point_ids, owner_count):
    tiles = cam_ids.shape[0]
    inputs = (owners, counts, direction, cam_ids, cam_jac, pt_jac, point_ids)
    spaces = [pltpu.SMEM] * 2 + [pltpu.VMEM] * 5
    return pl.pallas_call(
        pack_kernel,
        out_shape=(
            shape(owner_count * PER_OWNER * SLOT_ROWS, LANES),
            shape(tiles, owner_count * PER_OWNER),
        ),
        in_specs=[pl.BlockSpec(memory_space=pltpu.HBM)] * 7,
        out_specs=(VMEM, VMEM),
        scratch_shapes=[
            pltpu.SMEM((owner_count,), i32),
            pltpu.VMEM((tiles * SLOT_ROWS, LANES), f32),
        ]
        + [space(value.shape, value.dtype) for space, value in zip(spaces, inputs)]
        + [pltpu.SemaphoreType.DMA((7,))],
        compiler_params=pltpu.CompilerParams(vmem_limit_bytes=60 * 1024 * 1024),
        name="pack_tiles",
    )(*inputs)


def points(received, damping):
    slots = received.shape[0] // SLOT_ROWS
    uppers = damping.shape[0]
    return pl.pallas_call(
        point_kernel,
        out_shape=shape(slots * 2, LANES),
        in_specs=[VMEM] * 2,
        out_specs=VMEM,
        scratch_shapes=[
            pltpu.VMEM((PLACES * CHUNK * GROUP * TERM_ROWS, LANES), f32),
            pltpu.VMEM((2, uppers * TERM_ROWS, LANES), f32),
            pltpu.VMEM((6 * uppers, LANES), f32),
        ],
        compiler_params=LIMIT,
        name="solve_points",
    )(received, damping)


def cameras(places, remain, cam_jac, cam_ids, copies):
    tiles = cam_ids.shape[0]
    return pl.pallas_call(
        camera_kernel,
        out_shape=shape(copies * 18, LANES),
        in_specs=[VMEM] * 4,
        out_specs=VMEM,
        scratch_shapes=[
            pltpu.VMEM((tiles * TERM_ROWS, LANES), f32),
            pltpu.VMEM((2, tiles, LANES), f32),
        ],
        compiler_params=LIMIT,
        name="sum_cameras",
    )(places, remain, cam_jac, cam_ids)


def scalar_sums(received, residual, direction, damping, precond, owner_count):
    vector = shape(*residual.shape)
    return pl.pallas_call(
        scalar_kernel,
        out_shape=(vector, vector, vector, shape(owner_count, LANES)),
        in_specs=[VMEM] * 5,
        out_specs=(VMEM,) * 4,
        compiler_params=LIMIT,
        name="camera_scalars",
    )(received, residual, direction, damping, precond)


def finish(scalars, solution_in, residual, direction, image, first_z, slope):
    vector = shape(*residual.shape)
    return pl.pallas_call(
        final_kernel,
        out_shape=(vector,) * 3,
        in_specs=[VMEM] * 7,
        out_specs=(VMEM,) * 3,
        compiler_params=LIMIT,
        name="update_vectors",
    )(scalars, solution_in, residual, direction, image, first_z, slope)


def exchange(rows, axis, count):
    depth = rows.shape[0] // count
    sent = rows.reshape(count, depth, 1, LANES)
    got = lax.all_to_all(sent, axis, split_axis=0, concat_axis=0, tiled=True)
    return got.reshape(count * depth, LANES)


def body(
    solution,
    residual,
    direction,
    cam_damping,
    precond,
    pt_damping,
    cam_jac,
    pt_jac,
    cam_ids,
    point_ids,
    owners,
    valid_counts,
):
    owner_count = lax.axis_size("cam")
    copies = lax.axis_size("pt")
    cam_jac = cam_jac.transpose(1, 0, 2)
    pt_jac = pt_jac.transpose(1, 0, 2)
    payload, places = pack(
        owners.reshape(-1),
        valid_counts,
        direction,
        cam_ids,
        cam_jac,
        pt_jac,
        point_ids,
        owner_count,
    )
    received = exchange(payload, "cam", owner_count)
    remain = points(received, pt_damping.reshape(-1, POINT_LOW))
    returned = exchange(remain, "cam", owner_count)
    image_rows = cameras(places, returned, cam_jac, cam_ids, copies)
    image_all = exchange(image_rows, "pt", copies)
    image, first_z, slope, scalars = scalar_sums(
        image_all, residual, direction, cam_damping, precond, owner_count
    )
    scalars_all = exchange(scalars, "cam", owner_count)
    return finish(scalars_all, solution, residual, direction, image, first_z, slope)


def solution(mesh):
    return jax.shard_map(
        body,
        mesh=mesh,
        in_specs=(
            P(None, "cam"),
            P(None, "cam"),
            P(None, "cam"),
            P(None, "cam"),
            P(None, "cam"),
            P(("cam", "pt")),
            P(("cam", "pt"), None, None),
            P(("cam", "pt"), None, None),
            P(("cam", "pt"), None),
            P(("cam", "pt"), None),
            P(("cam", "pt"), None),
            P(("cam", "pt")),
        ),
        out_specs=(P(None, "cam"), P(None, "cam"), P(None, "cam")),
        check_vma=False,
    )
```

```python
import functools

import jax
import jax.numpy as jnp
from jax import lax
from jax.experimental import pallas as pl
from jax.experimental.pallas import tpu as pltpu
from jax.sharding import PartitionSpec as P

LANES = 128
PER_OWNER = 2
SLOT_ROWS = 8
TERM_ROWS = 32
GROUP = 8
POINT_LOW = 256
PARTS = 3
CHUNK = 2
PLACES = 4
WIDE = 2
CAM_CHUNK = 4

f32 = jnp.float32
bf16 = jnp.bfloat16
i32 = jnp.int32


def split(value):
    high = value.astype(bf16).astype(f32)
    rest = value - high
    middle = rest.astype(bf16).astype(f32)
    low = (rest - middle).astype(bf16).astype(f32)
    return high, middle, low


def lookup(table, index):
    return jnp.take_along_axis(table, index, axis=1, mode="promise_in_bounds")


def contract(left, right):
    return lax.dot_general(left, right, (((1,), (1,)), ((), ())), preferred_element_type=f32)


def store_terms(terms, values, group):
    base = group * GROUP * TERM_ROWS
    for term, value in enumerate(values):
        for part, piece in enumerate(split(value)):
            terms[pl.ds(base + part * 9 + term, GROUP, stride=TERM_ROWS), :] = piece


def one_hot(row_index, ids):
    return jnp.where(row_index == ids, jnp.ones((), bf16), jnp.zeros((), bf16))


def spread(value, s, rows):
    return jnp.broadcast_to(value[s : s + 1, :], (rows, LANES)).astype(bf16)


def turn_of(first, second):
    largest = jnp.maximum(jnp.abs(first), jnp.abs(second))
    zero = largest == 0.0
    scale = jnp.where(zero, 1.0, largest)
    along = jnp.where(zero, 1.0, first / scale)
    across = second / scale
    root = jnp.sqrt(along * along + across * across)
    return along / root, across / root, largest * root


def turn(cosine, sine, first, second):
    return cosine * first + sine * second, cosine * second - sine * first


def pack_kernel(*refs):
    sources, outputs, held, sem = refs[:7], refs[7:10], refs[12:19], refs[19]
    payload, places, turns = outputs
    seen, stage = refs[10:12]
    copies = [
        pltpu.make_async_copy(source, target, sem.at[k])
        for k, (source, target) in enumerate(zip(sources, held))
    ]
    for copy in copies:
        copy.start()
    payload[...] = jnp.zeros(payload.shape, f32)
    owners, counts, direction, cam_ids, cam_jac, pt_jac, point_ids = held
    tiles = cam_ids.shape[0]
    for index in range(seen.shape[0]):
        seen[index] = 0
    for copy in copies:
        copy.wait()
    lane = lax.broadcasted_iota(i32, (GROUP, LANES), 1)
    row = lax.broadcasted_iota(i32, (GROUP, LANES), 0)
    for group in range(tiles // GROUP):
        span = slice(group * GROUP, (group + 1) * GROUP)
        ids = cam_ids[span, :]
        low = ids & (LANES - 1)
        upper = ids >= LANES
        errors = [None, None]
        for j in range(9):
            tables = [
                jnp.broadcast_to(direction[j : j + 1, LANES * c : LANES * (c + 1)], (GROUP, LANES))
                for c in range(2)
            ]
            picked = jnp.where(upper, lookup(tables[1], low), lookup(tables[0], low))
            for r in range(2):
                term = cam_jac[9 * r + j, span, :] * picked
                errors[r] = term if errors[r] is None else errors[r] + term
        used = jnp.zeros((GROUP, LANES), i32)
        for s in range(GROUP):
            used = jnp.where(row == s, counts[group * GROUP + s], used)
        valid = lane < used
        jac = [jnp.where(valid, pt_jac[a, span, :], 0.0) for a in range(6)]
        errors = [jnp.where(valid, value, 0.0) for value in errors]
        cosine, sine, length = turn_of(jac[0], jac[3])
        turns[0, span, :] = cosine
        turns[1, span, :] = sine
        upper_row, lower_row = zip(
            *[turn(cosine, sine, jac[a], jac[3 + a]) for a in (1, 2)],
            turn(cosine, sine, *errors),
        )
        values = [length, upper_row[0], upper_row[1], lower_row[0], lower_row[1]]
        values += [upper_row[2], lower_row[2], point_ids[span, :].astype(f32)]
        for r, value in enumerate(values):
            stage[pl.ds(group * GROUP * SLOT_ROWS + r, GROUP, stride=SLOT_ROWS), :] = value
    slot_lane = lax.broadcasted_iota(i32, (1, places.shape[1]), 1)
    for tile in range(tiles):
        owner = owners[tile]
        rank = seen[owner]
        seen[owner] = rank + 1
        slot = owner * PER_OWNER + rank
        places[tile : tile + 1, :] = jnp.where(slot_lane == slot, 1.0, 0.0)
        payload[pl.ds(slot * SLOT_ROWS, SLOT_ROWS), :] = stage[
            tile * SLOT_ROWS : (tile + 1) * SLOT_ROWS, :
        ]


def solve_points(rhs, normal, damping):
    upper_aa = normal[0] + damping
    upper_ab = normal[1]
    upper_ac = normal[2]
    upper_bb = normal[3] + damping
    upper_bc = normal[4]
    upper_cc = normal[5] + damping
    minor_aa = upper_bb * upper_cc - upper_bc * upper_bc
    minor_ab = upper_ac * upper_bc - upper_ab * upper_cc
    minor_ac = upper_ab * upper_bc - upper_ac * upper_bb
    minor_bb = upper_aa * upper_cc - upper_ac * upper_ac
    minor_bc = upper_ab * upper_ac - upper_aa * upper_bc
    minor_cc = upper_aa * upper_bb - upper_ab * upper_ab
    determ = upper_aa * minor_aa + upper_ab * minor_ab + upper_ac * minor_ac
    return (
        (minor_aa * rhs[0] + minor_ab * rhs[1] + minor_ac * rhs[2]) / determ,
        (minor_ab * rhs[0] + minor_bb * rhs[1] + minor_bc * rhs[2]) / determ,
        (minor_ac * rhs[0] + minor_bc * rhs[1] + minor_cc * rhs[2]) / determ,
    )


def point_kernel(received, damping, remain, terms, sums, answers):
    slots = remain.shape[0] // 2
    groups = slots // GROUP
    uppers = damping.shape[0]
    rows = GROUP * SLOT_ROWS
    terms[...] = jnp.zeros(terms.shape, f32)
    sums[...] = jnp.zeros(sums.shape, f32)
    low_of_row = lax.broadcasted_iota(i32, (POINT_LOW, LANES), 0).astype(bf16)

    def chunk(start, place):
        lefts, rights = [], []
        for k in range(CHUNK):
            base = (start + k) * rows
            first = [received[pl.ds(base + r, GROUP, stride=SLOT_ROWS), :] for r in range(3)]
            second = [received[pl.ds(base + 3 + r, GROUP, stride=SLOT_ROWS), :] for r in range(2)]
            err0 = received[pl.ds(base + 5, GROUP, stride=SLOT_ROWS), :]
            err1 = received[pl.ds(base + 6, GROUP, stride=SLOT_ROWS), :]
            ids = received[pl.ds(base + 7, GROUP, stride=SLOT_ROWS), :].astype(i32)
            upper = (ids // POINT_LOW).astype(f32)
            lower = (ids & (POINT_LOW - 1)).astype(f32)
            values = [first[0] * err0]
            values += [first[a] * err0 + second[a - 1] * err1 for a in (1, 2)]
            values += [first[0] * first[a] for a in range(3)]
            for a, b in ((1, 1), (1, 2), (2, 2)):
                values.append(first[a] * first[b] + second[a - 1] * second[b - 1])
            store_terms(terms, values, place * CHUNK + k)
            for s in range(GROUP):
                at = ((place * CHUNK + k) * GROUP + s) * TERM_ROWS
                block = terms[at : at + TERM_ROWS, :].astype(bf16)
                upper_row = spread(upper, s, TERM_ROWS)
                lefts.append(
                    jnp.concatenate(
                        [
                            jnp.where(upper_row == jnp.asarray(h, bf16), block, jnp.zeros_like(block))
                            for h in range(uppers)
                        ],
                        axis=0,
                    )
                )
                rights.append(one_hot(low_of_row, spread(lower, s, POINT_LOW)))
        return contract(jnp.concatenate(lefts, axis=1), jnp.concatenate(rights, axis=1))

    @pl.loop(0, groups // (CHUNK * PLACES))
    def _(step):
        for place in range(PLACES):
            added = chunk((step * PLACES + place) * CHUNK, place)
            for half in range(2):
                sums[half] += added[:, half * LANES : (half + 1) * LANES]

    for half in range(2):
        columns = slice(half * LANES, (half + 1) * LANES)
        total = []
        for term in range(9):
            pieces = [
                sums[half, pl.ds(part * 9 + term, uppers, stride=TERM_ROWS), :]
                for part in range(PARTS)
            ]
            total.append(pieces[0] + (pieces[1] + pieces[2]))
        solved = solve_points(total[:3], total[3:], damping[:, columns])
        for a in range(3):
            answers[pl.ds((a * 2 + half) * uppers, uppers), :] = solved[a]

    @pl.loop(0, groups // WIDE)
    def _(step):
        bases = [(step * WIDE + w) * rows for w in range(WIDE)]
        ids = [
            received[pl.ds(base + 7, GROUP, stride=SLOT_ROWS), :].astype(i32) for base in bases
        ]
        lanes = [value & (LANES - 1) for value in ids]
        chunks = [value // LANES for value in ids]
        got = [[None] * 3 for _ in range(WIDE)]
        for k in range(2 * uppers):
            h, half = k // 2, k % 2
            for a in range(3):
                row = (a * 2 + half) * uppers + h
                table = jnp.broadcast_to(answers[row : row + 1, :], (GROUP, LANES))
                for w in range(WIDE):
                    value = lookup(table, lanes[w])
                    got[w][a] = value if k == 0 else jnp.where(chunks[w] == k, value, got[w][a])
        for w, base in enumerate(bases):
            rows_of = [received[pl.ds(base + r, GROUP, stride=SLOT_ROWS), :] for r in range(7)]
            y = got[w]
            images = [
                rows_of[0] * y[0] + (rows_of[1] * y[1] + rows_of[2] * y[2]),
                rows_of[3] * y[1] + rows_of[4] * y[2],
            ]
            for r in range(2):
                remain[pl.ds((step * WIDE + w) * 2 * GROUP + r, GROUP, stride=2), :] = (
                    rows_of[5 + r] - images[r]
                )


def camera_kernel(places, turns, remain, cam_jac, cam_ids, image, terms, stage):
    tiles = cam_ids.shape[0]
    cams = 2 * LANES
    copies = image.shape[0] // 18
    cam_of_row = lax.broadcasted_iota(i32, (cams, LANES), 0).astype(bf16)
    terms[...] = jnp.zeros(terms.shape, f32)
    chosen = places[...].astype(bf16)
    for r in range(2):
        high, middle, low = [
            lax.dot_general(
                chosen, piece.astype(bf16), (((1,), (0,)), ((), ())), preferred_element_type=f32
            )
            for piece in split(remain[pl.ds(r, places.shape[1], stride=2), :])
        ]
        stage[r] = high + (middle + low)
    total = None
    for start in range(0, tiles // GROUP, CAM_CHUNK):
        lefts, rights = [], []
        for group in range(start, start + CAM_CHUNK):
            span = slice(group * GROUP, (group + 1) * GROUP)
            cosine, sine = turns[0, span, :], turns[1, span, :]
            rest = turn(cosine, -sine, stage[0, span, :], stage[1, span, :])
            values = [
                cam_jac[j, span, :] * rest[0] + cam_jac[9 + j, span, :] * rest[1] for j in range(9)
            ]
            store_terms(terms, values, group)
            ids = cam_ids[span, :].astype(f32)
            for s in range(GROUP):
                at = (group * GROUP + s) * TERM_ROWS
                lefts.append(terms[at : at + TERM_ROWS, :].astype(bf16))
                rights.append(one_hot(cam_of_row, spread(ids, s, cams)))
        added = contract(jnp.concatenate(lefts, axis=1), jnp.concatenate(rights, axis=1))
        total = added if total is None else total + added
    for half in range(2):
        terms[0:TERM_ROWS, :] = total[:, half * LANES : (half + 1) * LANES]
        summed = terms[0:9, :] + (terms[9:18, :] + terms[18:27, :])
        for copy in range(copies):
            image[copy * 18 + half * 9 : copy * 18 + half * 9 + 9, :] = summed


def apply_blocks(precond, vector):
    total = None
    for j in range(9):
        term = precond[9 * j : 9 * j + 9, :] * vector[j : j + 1, :]
        total = term if total is None else total + term
    return total


def scalar_kernel(received, residual, direction, damping, precond, image, first_z, slope, scalars):
    copies = received.shape[0] // 18
    for half in range(2):
        columns = slice(half * LANES, (half + 1) * LANES)
        total = received[half * 9 : half * 9 + 9, :]
        for copy in range(1, copies):
            total = total + received[copy * 18 + half * 9 : copy * 18 + half * 9 + 9, :]
        image[:, columns] = damping[:, columns] * direction[:, columns] + total
    z = apply_blocks(precond, residual)
    y = apply_blocks(precond, image)
    first_z[...] = z
    slope[...] = y
    res = residual[...]
    img = image[...]
    sums = [
        jnp.sum(res * z),
        jnp.sum(direction[...] * img),
        jnp.sum(img * z + res * y),
        jnp.sum(img * y),
    ]
    lane = lax.broadcasted_iota(i32, scalars.shape, 1)
    row = jnp.zeros(scalars.shape, f32)
    for k, value in enumerate(sums):
        row = jnp.where(lane == k, value, row)
    scalars[...] = row


def final_kernel(
    scalars,
    solution_in,
    residual,
    direction,
    image,
    first_z,
    slope,
    new_solution,
    new_residual,
    new_direction,
):
    total = jnp.sum(scalars[...], axis=0, keepdims=True)
    lane = lax.broadcasted_iota(i32, total.shape, 1)
    rz, pq, cross, square = [
        jnp.sum(jnp.where(lane == k, total, 0.0), axis=1, keepdims=True) for k in range(4)
    ]
    alpha = rz / pq
    rz1 = rz + alpha * (alpha * square - cross)
    way = direction[...]
    new_solution[...] = solution_in[...] + alpha * way
    new_residual[...] = residual[...] - alpha * image[...]
    new_direction[...] = first_z[...] - alpha * slope[...] + (rz1 / rz) * way


SMEM = pl.BlockSpec(memory_space=pltpu.SMEM)
VMEM = pl.BlockSpec(memory_space=pltpu.VMEM)
LIMIT = pltpu.CompilerParams(vmem_limit_bytes=32 * 1024 * 1024)


def shape(*dims, dtype=f32):
    return jax.ShapeDtypeStruct(dims, dtype)


def pack(owners, counts, direction, cam_ids, cam_jac, pt_jac, point_ids, owner_count):
    tiles = cam_ids.shape[0]
    inputs = (owners, counts, direction, cam_ids, cam_jac, pt_jac, point_ids)
    spaces = [pltpu.SMEM] * 2 + [pltpu.VMEM] * 5
    return pl.pallas_call(
        pack_kernel,
        out_shape=(
            pltpu.VMEM((owner_count * PER_OWNER * SLOT_ROWS, LANES), f32),
            pltpu.VMEM((tiles, owner_count * PER_OWNER), f32),
            pltpu.VMEM((2, tiles, LANES), f32),
        ),
        in_specs=[pl.BlockSpec(memory_space=pltpu.HBM)] * 7,
        out_specs=(VMEM,) * 3,
        scratch_shapes=[
            pltpu.SMEM((owner_count,), i32),
            pltpu.VMEM((tiles * SLOT_ROWS, LANES), f32),
        ]
        + [space(value.shape, value.dtype) for space, value in zip(spaces, inputs)]
        + [pltpu.SemaphoreType.DMA((7,))],
        compiler_params=pltpu.CompilerParams(vmem_limit_bytes=60 * 1024 * 1024),
        name="pack_tiles",
    )(*inputs)


def points(received, damping):
    slots = received.shape[0] // SLOT_ROWS
    uppers = damping.shape[0]
    return pl.pallas_call(
        point_kernel,
        out_shape=shape(slots * 2, LANES),
        in_specs=[VMEM] * 2,
        out_specs=VMEM,
        scratch_shapes=[
            pltpu.VMEM((PLACES * CHUNK * GROUP * TERM_ROWS, LANES), f32),
            pltpu.VMEM((2, uppers * TERM_ROWS, LANES), f32),
            pltpu.VMEM((6 * uppers, LANES), f32),
        ],
        compiler_params=LIMIT,
        name="solve_points",
    )(received, damping)


def cameras(places, turns, remain, cam_jac, cam_ids, copies):
    tiles = cam_ids.shape[0]
    return pl.pallas_call(
        camera_kernel,
        out_shape=shape(copies * 18, LANES),
        in_specs=[VMEM] * 5,
        out_specs=VMEM,
        scratch_shapes=[
            pltpu.VMEM((tiles * TERM_ROWS, LANES), f32),
            pltpu.VMEM((2, tiles, LANES), f32),
        ],
        compiler_params=LIMIT,
        name="sum_cameras",
    )(places, turns, remain, cam_jac, cam_ids)


def scalar_sums(received, residual, direction, damping, precond, owner_count):
    vector = shape(*residual.shape)
    return pl.pallas_call(
        scalar_kernel,
        out_shape=(vector, vector, vector, shape(owner_count, LANES)),
        in_specs=[VMEM] * 5,
        out_specs=(VMEM,) * 4,
        compiler_params=LIMIT,
        name="camera_scalars",
    )(received, residual, direction, damping, precond)


def finish(scalars, solution_in, residual, direction, image, first_z, slope):
    vector = shape(*residual.shape)
    return pl.pallas_call(
        final_kernel,
        out_shape=(vector,) * 3,
        in_specs=[VMEM] * 7,
        out_specs=(VMEM,) * 3,
        compiler_params=LIMIT,
        name="update_vectors",
    )(scalars, solution_in, residual, direction, image, first_z, slope)


def exchange(rows, axis, count):
    depth = rows.shape[0] // count
    sent = rows.reshape(count, depth, 1, LANES)
    got = lax.all_to_all(sent, axis, split_axis=0, concat_axis=0, tiled=True)
    return got.reshape(count * depth, LANES)


def body(
    solution,
    residual,
    direction,
    cam_damping,
    precond,
    pt_damping,
    cam_jac,
    pt_jac,
    cam_ids,
    point_ids,
    owners,
    valid_counts,
):
    owner_count = lax.axis_size("cam")
    copies = lax.axis_size("pt")
    cam_jac = cam_jac.transpose(1, 0, 2)
    pt_jac = pt_jac.transpose(1, 0, 2)
    payload, places, turns = pack(
        owners.reshape(-1),
        valid_counts,
        direction,
        cam_ids,
        cam_jac,
        pt_jac,
        point_ids,
        owner_count,
    )
    received = exchange(payload, "cam", owner_count)
    remain = points(received, pt_damping.reshape(-1, POINT_LOW))
    returned = exchange(remain, "cam", owner_count)
    image_rows = cameras(places, turns, returned, cam_jac, cam_ids, copies)
    image_all = exchange(image_rows, "pt", copies)
    image, first_z, slope, scalars = scalar_sums(
        image_all, residual, direction, cam_damping, precond, owner_count
    )
    scalars_all = exchange(scalars, "cam", owner_count)
    return finish(scalars_all, solution, residual, direction, image, first_z, slope)


def solution(mesh):
    return jax.shard_map(
        body,
        mesh=mesh,
        in_specs=(
            P(None, "cam"),
            P(None, "cam"),
            P(None, "cam"),
            P(None, "cam"),
            P(None, "cam"),
            P(("cam", "pt")),
            P(("cam", "pt"), None, None),
            P(("cam", "pt"), None, None),
            P(("cam", "pt"), None),
            P(("cam", "pt"), None),
            P(("cam", "pt"), None),
            P(("cam", "pt")),
        ),
        out_specs=(P(None, "cam"), P(None, "cam"), P(None, "cam")),
        check_vma=False,
    )
```

```python
import functools

import jax
import jax.numpy as jnp
from jax import lax
from jax.experimental import pallas as pl
from jax.experimental.pallas import tpu as pltpu
from jax.sharding import PartitionSpec as P

LANES = 128
PER_OWNER = 2
SLOT_ROWS = 8
TERM_ROWS = 32
GROUP = 8
POINT_LOW = 256
PARTS = 3
CHUNK = 2
PLACES = 8
WIDE = 2
CAM_CHUNK = 2

f32 = jnp.float32
bf16 = jnp.bfloat16
i32 = jnp.int32


def split(value):
    high = value.astype(bf16).astype(f32)
    rest = value - high
    middle = rest.astype(bf16).astype(f32)
    low = (rest - middle).astype(bf16).astype(f32)
    return high, middle, low


def lookup(table, index):
    return jnp.take_along_axis(table, index, axis=1, mode="promise_in_bounds")


def contract(left, right):
    return lax.dot_general(left, right, (((1,), (1,)), ((), ())), preferred_element_type=f32)


def store_terms(terms, values, group):
    base = group * GROUP * TERM_ROWS
    for term, value in enumerate(values):
        for part, piece in enumerate(split(value)):
            terms[pl.ds(base + part * 9 + term, GROUP, stride=TERM_ROWS), :] = piece


def one_hot(row_index, ids):
    return jnp.where(row_index == ids, jnp.ones((), bf16), jnp.zeros((), bf16))


def by_upper(block, upper_row, uppers):
    zero = jnp.zeros_like(block)
    return jnp.concatenate(
        [jnp.where(upper_row == jnp.asarray(h, bf16), block, zero) for h in range(uppers)], axis=0
    )


def spread(value, s, rows):
    return jnp.broadcast_to(value[s : s + 1, :], (rows, LANES)).astype(bf16)


def turn_of(first, second):
    largest = jnp.maximum(jnp.abs(first), jnp.abs(second))
    zero = largest == 0.0
    scale = jnp.where(zero, 1.0, largest)
    along = jnp.where(zero, 1.0, first / scale)
    across = second / scale
    root = jnp.sqrt(along * along + across * across)
    return along / root, across / root, largest * root


def turn(cosine, sine, first, second):
    return cosine * first + sine * second, cosine * second - sine * first


def pack_kernel(*refs):
    sources, outputs, held, sem = refs[:7], refs[7:10], refs[12:19], refs[19]
    payload, places, turns = outputs
    seen, stage = refs[10:12]
    copies = [
        pltpu.make_async_copy(source, target, sem.at[k])
        for k, (source, target) in enumerate(zip(sources, held))
    ]
    for copy in copies:
        copy.start()
    payload[...] = jnp.zeros(payload.shape, f32)
    owners, counts, direction, cam_ids, cam_jac, pt_jac, point_ids = held
    tiles = cam_ids.shape[0]
    for index in range(seen.shape[0]):
        seen[index] = 0
    for copy in copies:
        copy.wait()
    lane = lax.broadcasted_iota(i32, (GROUP, LANES), 1)
    row = lax.broadcasted_iota(i32, (GROUP, LANES), 0)
    for group in range(tiles // GROUP):
        span = slice(group * GROUP, (group + 1) * GROUP)
        ids = cam_ids[span, :]
        low = ids & (LANES - 1)
        upper = ids >= LANES
        errors = [None, None]
        for j in range(9):
            tables = [
                jnp.broadcast_to(direction[j : j + 1, LANES * c : LANES * (c + 1)], (GROUP, LANES))
                for c in range(2)
            ]
            picked = jnp.where(upper, lookup(tables[1], low), lookup(tables[0], low))
            for r in range(2):
                term = cam_jac[9 * r + j, span, :] * picked
                errors[r] = term if errors[r] is None else errors[r] + term
        used = jnp.zeros((GROUP, LANES), i32)
        for s in range(GROUP):
            used = jnp.where(row == s, counts[group * GROUP + s], used)
        valid = lane < used
        jac = [jnp.where(valid, pt_jac[a, span, :], 0.0) for a in range(6)]
        errors = [jnp.where(valid, value, 0.0) for value in errors]
        cosine, sine, length = turn_of(jac[0], jac[3])
        turns[0, span, :] = cosine
        turns[1, span, :] = sine
        upper_row, lower_row = zip(
            *[turn(cosine, sine, jac[a], jac[3 + a]) for a in (1, 2)],
            turn(cosine, sine, *errors),
        )
        values = [length, upper_row[0], upper_row[1], lower_row[0], lower_row[1]]
        values += [upper_row[2], lower_row[2], point_ids[span, :].astype(f32)]
        for r, value in enumerate(values):
            stage[pl.ds(group * GROUP * SLOT_ROWS + r, GROUP, stride=SLOT_ROWS), :] = value
    slot_lane = lax.broadcasted_iota(i32, (1, places.shape[1]), 1)
    for tile in range(tiles):
        owner = owners[tile]
        rank = seen[owner]
        seen[owner] = rank + 1
        slot = owner * PER_OWNER + rank
        places[tile : tile + 1, :] = jnp.where(slot_lane == slot, 1.0, 0.0)
        payload[pl.ds(slot * SLOT_ROWS, SLOT_ROWS), :] = stage[
            tile * SLOT_ROWS : (tile + 1) * SLOT_ROWS, :
        ]


def solve_points(rhs, normal, damping):
    upper_aa = normal[0] + damping
    upper_ab = normal[1]
    upper_ac = normal[2]
    upper_bb = normal[3] + damping
    upper_bc = normal[4]
    upper_cc = normal[5] + damping
    minor_aa = upper_bb * upper_cc - upper_bc * upper_bc
    minor_ab = upper_ac * upper_bc - upper_ab * upper_cc
    minor_ac = upper_ab * upper_bc - upper_ac * upper_bb
    minor_bb = upper_aa * upper_cc - upper_ac * upper_ac
    minor_bc = upper_ab * upper_ac - upper_aa * upper_bc
    minor_cc = upper_aa * upper_bb - upper_ab * upper_ab
    determ = upper_aa * minor_aa + upper_ab * minor_ab + upper_ac * minor_ac
    return (
        (minor_aa * rhs[0] + minor_ab * rhs[1] + minor_ac * rhs[2]) / determ,
        (minor_ab * rhs[0] + minor_bb * rhs[1] + minor_bc * rhs[2]) / determ,
        (minor_ac * rhs[0] + minor_bc * rhs[1] + minor_cc * rhs[2]) / determ,
    )


def point_kernel(received, damping, remain, terms, sums, answers):
    slots = remain.shape[0] // 2
    groups = slots // GROUP
    uppers = damping.shape[0] // 2
    rows = GROUP * SLOT_ROWS
    sums[...] = jnp.zeros(sums.shape, f32)
    low_of_row = lax.broadcasted_iota(i32, (POINT_LOW, LANES), 0).astype(bf16)

    def chunk(start, place):
        lefts, rights = [], []
        for k in range(CHUNK):
            base = (start + k) * rows
            first = [received[pl.ds(base + r, GROUP, stride=SLOT_ROWS), :] for r in range(3)]
            second = [received[pl.ds(base + 3 + r, GROUP, stride=SLOT_ROWS), :] for r in range(2)]
            err0 = received[pl.ds(base + 5, GROUP, stride=SLOT_ROWS), :]
            err1 = received[pl.ds(base + 6, GROUP, stride=SLOT_ROWS), :]
            ids = received[pl.ds(base + 7, GROUP, stride=SLOT_ROWS), :].astype(i32)
            upper = (ids // POINT_LOW).astype(f32)
            lower = (ids & (POINT_LOW - 1)).astype(f32)
            values = [first[0] * err0]
            values += [first[a] * err0 + second[a - 1] * err1 for a in (1, 2)]
            values += [first[0] * first[a] for a in range(3)]
            for a, b in ((1, 1), (1, 2), (2, 2)):
                values.append(first[a] * first[b] + second[a - 1] * second[b - 1])
            store_terms(terms, values, place * CHUNK + k)
            for s in range(GROUP):
                at = ((place * CHUNK + k) * GROUP + s) * TERM_ROWS
                block = terms[at : at + TERM_ROWS, :].astype(bf16)
                upper_row = spread(upper, s, TERM_ROWS)
                lefts.append(by_upper(block, upper_row, uppers))
                rights.append(one_hot(low_of_row, spread(lower, s, POINT_LOW)))
        return contract(jnp.concatenate(lefts, axis=1), jnp.concatenate(rights, axis=1))

    @pl.loop(0, groups // (CHUNK * PLACES))
    def _(step):
        for place in range(PLACES):
            added = chunk((step * PLACES + place) * CHUNK, place)
            for half in range(2):
                sums[half] += added[:, half * LANES : (half + 1) * LANES]

    for half in range(2):
        total = []
        for term in range(9):
            pieces = [
                sums[half, pl.ds(part * 9 + term, uppers, stride=TERM_ROWS), :]
                for part in range(PARTS)
            ]
            total.append(pieces[0] + (pieces[1] + pieces[2]))
        solved = solve_points(total[:3], total[3:], damping[pl.ds(half, uppers, stride=2), :])
        for a in range(3):
            for h in range(uppers):
                row = ((a * 2 + half) * uppers + h) * GROUP
                answers[row : row + GROUP, :] = jnp.broadcast_to(
                    solved[a][h : h + 1, :], (GROUP, LANES)
                )

    @pl.loop(0, groups // WIDE)
    def _(step):
        bases = [(step * WIDE + w) * rows for w in range(WIDE)]
        ids = [
            received[pl.ds(base + 7, GROUP, stride=SLOT_ROWS), :].astype(i32) for base in bases
        ]
        lanes = [value & (LANES - 1) for value in ids]
        chunks = [value // LANES for value in ids]
        got = [[None] * 3 for _ in range(WIDE)]
        for k in range(2 * uppers):
            h, half = k // 2, k % 2
            for a in range(3):
                row = ((a * 2 + half) * uppers + h) * GROUP
                table = answers[row : row + GROUP, :]
                for w in range(WIDE):
                    value = lookup(table, lanes[w])
                    got[w][a] = value if k == 0 else jnp.where(chunks[w] == k, value, got[w][a])
        for w, base in enumerate(bases):
            rows_of = [received[pl.ds(base + r, GROUP, stride=SLOT_ROWS), :] for r in range(7)]
            y = got[w]
            images = [
                rows_of[0] * y[0] + (rows_of[1] * y[1] + rows_of[2] * y[2]),
                rows_of[3] * y[1] + rows_of[4] * y[2],
            ]
            for r in range(2):
                remain[pl.ds((step * WIDE + w) * 2 * GROUP + r, GROUP, stride=2), :] = (
                    rows_of[5 + r] - images[r]
                )


def camera_kernel(places, turns, remain, cam_jac, cam_ids, image, terms, stage):
    tiles = cam_ids.shape[0]
    copies = image.shape[0] // 18
    low_of_row = lax.broadcasted_iota(i32, (LANES, LANES), 0).astype(bf16)
    chosen = places[...].astype(bf16)
    for r in range(2):
        high, middle, low = [
            lax.dot_general(
                chosen, piece.astype(bf16), (((1,), (0,)), ((), ())), preferred_element_type=f32
            )
            for piece in split(remain[pl.ds(r, places.shape[1], stride=2), :])
        ]
        stage[r] = high + (middle + low)
    total = None
    for start in range(0, tiles // GROUP, CAM_CHUNK):
        lefts, rights = [], []
        for group in range(start, start + CAM_CHUNK):
            span = slice(group * GROUP, (group + 1) * GROUP)
            cosine, sine = turns[0, span, :], turns[1, span, :]
            rest = turn(cosine, -sine, stage[0, span, :], stage[1, span, :])
            values = [
                cam_jac[j, span, :] * rest[0] + cam_jac[9 + j, span, :] * rest[1] for j in range(9)
            ]
            store_terms(terms, values, group)
            ids = cam_ids[span, :]
            upper = (ids // LANES).astype(f32)
            lower = (ids & (LANES - 1)).astype(f32)
            for s in range(GROUP):
                at = (group * GROUP + s) * TERM_ROWS
                block = terms[at : at + TERM_ROWS, :].astype(bf16)
                lefts.append(by_upper(block, spread(upper, s, TERM_ROWS), 2))
                rights.append(one_hot(low_of_row, spread(lower, s, LANES)))
        added = contract(jnp.concatenate(lefts, axis=1), jnp.concatenate(rights, axis=1))
        total = added if total is None else total + added
    for half in range(2):
        terms[0:TERM_ROWS, :] = total[half * TERM_ROWS : (half + 1) * TERM_ROWS, :]
        summed = terms[0:9, :] + (terms[9:18, :] + terms[18:27, :])
        for copy in range(copies):
            image[copy * 18 + half * 9 : copy * 18 + half * 9 + 9, :] = summed


def apply_blocks(precond, vector):
    total = None
    for j in range(9):
        term = precond[9 * j : 9 * j + 9, :] * vector[j : j + 1, :]
        total = term if total is None else total + term
    return total


def scalar_kernel(received, residual, direction, damping, precond, image, first_z, slope, scalars):
    copies = received.shape[0] // 18
    for half in range(2):
        columns = slice(half * LANES, (half + 1) * LANES)
        total = received[half * 9 : half * 9 + 9, :]
        for copy in range(1, copies):
            total = total + received[copy * 18 + half * 9 : copy * 18 + half * 9 + 9, :]
        image[:, columns] = damping[:, columns] * direction[:, columns] + total
    z = apply_blocks(precond, residual)
    y = apply_blocks(precond, image)
    first_z[...] = z
    slope[...] = y
    res = residual[...]
    img = image[...]
    sums = [
        jnp.sum(res * z),
        jnp.sum(direction[...] * img),
        jnp.sum(img * z + res * y),
        jnp.sum(img * y),
    ]
    lane = lax.broadcasted_iota(i32, scalars.shape, 1)
    row = jnp.zeros(scalars.shape, f32)
    for k, value in enumerate(sums):
        row = jnp.where(lane == k, value, row)
    scalars[...] = row


def final_kernel(
    scalars,
    solution_in,
    residual,
    direction,
    image,
    first_z,
    slope,
    new_solution,
    new_residual,
    new_direction,
):
    total = jnp.sum(scalars[...], axis=0, keepdims=True)
    lane = lax.broadcasted_iota(i32, total.shape, 1)
    rz, pq, cross, square = [
        jnp.sum(jnp.where(lane == k, total, 0.0), axis=1, keepdims=True) for k in range(4)
    ]
    alpha = rz / pq
    rz1 = rz + alpha * (alpha * square - cross)
    way = direction[...]
    new_solution[...] = solution_in[...] + alpha * way
    new_residual[...] = residual[...] - alpha * image[...]
    new_direction[...] = first_z[...] - alpha * slope[...] + (rz1 / rz) * way


SMEM = pl.BlockSpec(memory_space=pltpu.SMEM)
VMEM = pl.BlockSpec(memory_space=pltpu.VMEM)
LIMIT = pltpu.CompilerParams(vmem_limit_bytes=32 * 1024 * 1024)


def shape(*dims, dtype=f32):
    return jax.ShapeDtypeStruct(dims, dtype)


def pack(owners, counts, direction, cam_ids, cam_jac, pt_jac, point_ids, owner_count):
    tiles = cam_ids.shape[0]
    inputs = (owners, counts, direction, cam_ids, cam_jac, pt_jac, point_ids)
    spaces = [pltpu.SMEM] * 2 + [pltpu.VMEM] * 5
    return pl.pallas_call(
        pack_kernel,
        out_shape=(
            pltpu.VMEM((owner_count * PER_OWNER * SLOT_ROWS, LANES), f32),
            pltpu.VMEM((tiles, owner_count * PER_OWNER), f32),
            pltpu.VMEM((2, tiles, LANES), f32),
        ),
        in_specs=[pl.BlockSpec(memory_space=pltpu.HBM)] * 7,
        out_specs=(VMEM,) * 3,
        scratch_shapes=[
            pltpu.SMEM((owner_count,), i32),
            pltpu.VMEM((tiles * SLOT_ROWS, LANES), f32),
        ]
        + [space(value.shape, value.dtype) for space, value in zip(spaces, inputs)]
        + [pltpu.SemaphoreType.DMA((7,))],
        compiler_params=pltpu.CompilerParams(vmem_limit_bytes=60 * 1024 * 1024),
        name="pack_tiles",
    )(*inputs)


def points(received, damping):
    slots = received.shape[0] // SLOT_ROWS
    uppers = damping.shape[0] // 2
    return pl.pallas_call(
        point_kernel,
        out_shape=shape(slots * 2, LANES),
        in_specs=[VMEM] * 2,
        out_specs=VMEM,
        scratch_shapes=[
            pltpu.VMEM((PLACES * CHUNK * GROUP * TERM_ROWS, LANES), f32),
            pltpu.VMEM((2, uppers * TERM_ROWS, LANES), f32),
            pltpu.VMEM((6 * uppers * GROUP, LANES), f32),
        ],
        compiler_params=LIMIT,
        name="solve_points",
    )(received, damping)


def cameras(places, turns, remain, cam_jac, cam_ids, copies):
    tiles = cam_ids.shape[0]
    return pl.pallas_call(
        camera_kernel,
        out_shape=shape(copies * 18, LANES),
        in_specs=[VMEM] * 5,
        out_specs=VMEM,
        scratch_shapes=[
            pltpu.VMEM((tiles * TERM_ROWS, LANES), f32),
            pltpu.VMEM((2, tiles, LANES), f32),
        ],
        compiler_params=LIMIT,
        name="sum_cameras",
    )(places, turns, remain, cam_jac, cam_ids)


def scalar_sums(received, residual, direction, damping, precond, owner_count):
    vector = shape(*residual.shape)
    return pl.pallas_call(
        scalar_kernel,
        out_shape=(vector, vector, vector, shape(owner_count, LANES)),
        in_specs=[VMEM] * 5,
        out_specs=(VMEM,) * 4,
        compiler_params=LIMIT,
        name="camera_scalars",
    )(received, residual, direction, damping, precond)


def finish(scalars, solution_in, residual, direction, image, first_z, slope):
    vector = shape(*residual.shape)
    return pl.pallas_call(
        final_kernel,
        out_shape=(vector,) * 3,
        in_specs=[VMEM] * 7,
        out_specs=(VMEM,) * 3,
        compiler_params=LIMIT,
        name="update_vectors",
    )(scalars, solution_in, residual, direction, image, first_z, slope)


def exchange(rows, axis, count):
    depth = rows.shape[0] // count
    sent = rows.reshape(count, depth, 1, LANES)
    got = lax.all_to_all(sent, axis, split_axis=0, concat_axis=0, tiled=True)
    return got.reshape(count * depth, LANES)


def body(
    solution,
    residual,
    direction,
    cam_damping,
    precond,
    pt_damping,
    cam_jac,
    pt_jac,
    cam_ids,
    point_ids,
    owners,
    valid_counts,
):
    owner_count = lax.axis_size("cam")
    copies = lax.axis_size("pt")
    cam_jac = cam_jac.transpose(1, 0, 2)
    pt_jac = pt_jac.transpose(1, 0, 2)
    payload, places, turns = pack(
        owners.reshape(-1),
        valid_counts,
        direction,
        cam_ids,
        cam_jac,
        pt_jac,
        point_ids,
        owner_count,
    )
    received = exchange(payload, "cam", owner_count)
    remain = points(received, pt_damping.reshape(-1, LANES))
    returned = exchange(remain, "cam", owner_count)
    image_rows = cameras(places, turns, returned, cam_jac, cam_ids, copies)
    image_all = exchange(image_rows, "pt", copies)
    image, first_z, slope, scalars = scalar_sums(
        image_all, residual, direction, cam_damping, precond, owner_count
    )
    scalars_all = exchange(scalars, "cam", owner_count)
    return finish(scalars_all, solution, residual, direction, image, first_z, slope)


def solution(mesh):
    return jax.shard_map(
        body,
        mesh=mesh,
        in_specs=(
            P(None, "cam"),
            P(None, "cam"),
            P(None, "cam"),
            P(None, "cam"),
            P(None, "cam"),
            P(("cam", "pt")),
            P(("cam", "pt"), None, None),
            P(("cam", "pt"), None, None),
            P(("cam", "pt"), None),
            P(("cam", "pt"), None),
            P(("cam", "pt"), None),
            P(("cam", "pt")),
        ),
        out_specs=(P(None, "cam"), P(None, "cam"), P(None, "cam")),
        check_vma=False,
    )
```

```python
import functools

import jax
import jax.numpy as jnp
from jax import lax
from jax.experimental import pallas as pl
from jax.experimental.pallas import tpu as pltpu
from jax.sharding import PartitionSpec as P

LANES = 128
PER_OWNER = 2
SLOT_ROWS = 8
TERM_ROWS = 32
GROUP = 8
POINT_LOW = 256
PARTS = 3
CHUNK = 2
PLACES = 8
WIDE = 8
CAM_CHUNK = 2

f32 = jnp.float32
bf16 = jnp.bfloat16
i32 = jnp.int32


def split(value):
    high = value.astype(bf16).astype(f32)
    rest = value - high
    middle = rest.astype(bf16).astype(f32)
    low = (rest - middle).astype(bf16).astype(f32)
    return high, middle, low


def lookup(table, index):
    return jnp.take_along_axis(table, index, axis=1, mode="promise_in_bounds")


def contract(left, right):
    return lax.dot_general(left, right, (((1,), (1,)), ((), ())), preferred_element_type=f32)


def store_terms(terms, values, group):
    base = group * GROUP * TERM_ROWS
    for term, value in enumerate(values):
        for part, piece in enumerate(split(value)):
            at = base + (part * 9 + term) * GROUP
            terms[at : at + GROUP, :] = piece


def slot_terms(terms, group, s):
    rows = pl.ds(group * GROUP * TERM_ROWS + s, TERM_ROWS, stride=GROUP)
    return terms[rows, :].astype(bf16)


def one_hot(row_index, ids):
    return jnp.where(row_index == ids, jnp.ones((), bf16), jnp.zeros((), bf16))


def by_upper(block, upper_row, uppers):
    zero = jnp.zeros_like(block)
    return jnp.concatenate(
        [jnp.where(upper_row == jnp.asarray(h, bf16), block, zero) for h in range(uppers)], axis=0
    )


def spread(value, s, rows):
    return jnp.broadcast_to(value[s : s + 1, :], (rows, LANES)).astype(bf16)


def turn_of(first, second):
    largest = jnp.maximum(jnp.abs(first), jnp.abs(second))
    zero = largest == 0.0
    scale = jnp.where(zero, 1.0, largest)
    along = jnp.where(zero, 1.0, first / scale)
    across = second / scale
    root = jnp.sqrt(along * along + across * across)
    return along / root, across / root, largest * root


def turn(cosine, sine, first, second):
    return cosine * first + sine * second, cosine * second - sine * first


def pack_kernel(*refs):
    sources, outputs, held, sem = refs[:7], refs[7:10], refs[12:19], refs[19]
    payload, places, turns = outputs
    seen, stage = refs[10:12]
    copies = [
        pltpu.make_async_copy(source, target, sem.at[k])
        for k, (source, target) in enumerate(zip(sources, held))
    ]
    for copy in copies:
        copy.start()
    payload[...] = jnp.zeros(payload.shape, f32)
    owners, counts, direction, cam_ids, cam_jac, pt_jac, point_ids = held
    tiles = cam_ids.shape[0]
    for index in range(seen.shape[0]):
        seen[index] = 0
    for copy in copies:
        copy.wait()
    lane = lax.broadcasted_iota(i32, (GROUP, LANES), 1)
    row = lax.broadcasted_iota(i32, (GROUP, LANES), 0)
    for group in range(tiles // GROUP):
        span = slice(group * GROUP, (group + 1) * GROUP)
        ids = cam_ids[span, :]
        low = ids & (LANES - 1)
        upper = ids >= LANES
        errors = [None, None]
        for j in range(9):
            tables = [
                jnp.broadcast_to(direction[j : j + 1, LANES * c : LANES * (c + 1)], (GROUP, LANES))
                for c in range(2)
            ]
            picked = jnp.where(upper, lookup(tables[1], low), lookup(tables[0], low))
            for r in range(2):
                term = cam_jac[9 * r + j, span, :] * picked
                errors[r] = term if errors[r] is None else errors[r] + term
        used = jnp.zeros((GROUP, LANES), i32)
        for s in range(GROUP):
            used = jnp.where(row == s, counts[group * GROUP + s], used)
        valid = lane < used
        jac = [jnp.where(valid, pt_jac[a, span, :], 0.0) for a in range(6)]
        errors = [jnp.where(valid, value, 0.0) for value in errors]
        cosine, sine, length = turn_of(jac[0], jac[3])
        turns[0, span, :] = cosine
        turns[1, span, :] = sine
        upper_row, lower_row = zip(
            *[turn(cosine, sine, jac[a], jac[3 + a]) for a in (1, 2)],
            turn(cosine, sine, *errors),
        )
        values = [length, upper_row[0], upper_row[1], lower_row[0], lower_row[1]]
        values += [upper_row[2], lower_row[2], point_ids[span, :].astype(f32)]
        for r, value in enumerate(values):
            at = (group * SLOT_ROWS + r) * GROUP
            stage[at : at + GROUP, :] = value
    slot_lane = lax.broadcasted_iota(i32, (1, places.shape[1]), 1)
    for tile in range(tiles):
        owner = owners[tile]
        rank = seen[owner]
        seen[owner] = rank + 1
        slot = owner * PER_OWNER + rank
        places[tile : tile + 1, :] = jnp.where(slot_lane == slot, 1.0, 0.0)
        at = tile // GROUP * GROUP * SLOT_ROWS + tile % GROUP
        payload[pl.ds(slot * SLOT_ROWS, SLOT_ROWS), :] = stage[
            pl.ds(at, SLOT_ROWS, stride=GROUP), :
        ]


def solve_points(rhs, normal, damping):
    upper_aa = normal[0] + damping
    upper_ab = normal[1]
    upper_ac = normal[2]
    upper_bb = normal[3] + damping
    upper_bc = normal[4]
    upper_cc = normal[5] + damping
    minor_aa = upper_bb * upper_cc - upper_bc * upper_bc
    minor_ab = upper_ac * upper_bc - upper_ab * upper_cc
    minor_ac = upper_ab * upper_bc - upper_ac * upper_bb
    minor_bb = upper_aa * upper_cc - upper_ac * upper_ac
    minor_bc = upper_ab * upper_ac - upper_aa * upper_bc
    minor_cc = upper_aa * upper_bb - upper_ab * upper_ab
    determ = upper_aa * minor_aa + upper_ab * minor_ab + upper_ac * minor_ac
    return (
        (minor_aa * rhs[0] + minor_ab * rhs[1] + minor_ac * rhs[2]) / determ,
        (minor_ab * rhs[0] + minor_bb * rhs[1] + minor_bc * rhs[2]) / determ,
        (minor_ac * rhs[0] + minor_bc * rhs[1] + minor_cc * rhs[2]) / determ,
    )


def point_kernel(received, damping, remain, terms, sums, answers):
    slots = remain.shape[0] // 2
    groups = slots // GROUP
    uppers = damping.shape[0] // 2
    rows = GROUP * SLOT_ROWS
    sums[...] = jnp.zeros(sums.shape, f32)
    low_of_row = lax.broadcasted_iota(i32, (POINT_LOW, LANES), 0).astype(bf16)

    def chunk(start, place):
        lefts, rights = [], []
        for k in range(CHUNK):
            base = (start + k) * rows
            first = [received[pl.ds(base + r, GROUP, stride=SLOT_ROWS), :] for r in range(3)]
            second = [received[pl.ds(base + 3 + r, GROUP, stride=SLOT_ROWS), :] for r in range(2)]
            err0 = received[pl.ds(base + 5, GROUP, stride=SLOT_ROWS), :]
            err1 = received[pl.ds(base + 6, GROUP, stride=SLOT_ROWS), :]
            ids = received[pl.ds(base + 7, GROUP, stride=SLOT_ROWS), :].astype(i32)
            upper = (ids // POINT_LOW).astype(f32)
            lower = (ids & (POINT_LOW - 1)).astype(f32)
            values = [first[0] * err0]
            values += [first[a] * err0 + second[a - 1] * err1 for a in (1, 2)]
            values += [first[0] * first[a] for a in range(3)]
            for a, b in ((1, 1), (1, 2), (2, 2)):
                values.append(first[a] * first[b] + second[a - 1] * second[b - 1])
            store_terms(terms, values, place * CHUNK + k)
            for s in range(GROUP):
                block = slot_terms(terms, place * CHUNK + k, s)
                upper_row = spread(upper, s, TERM_ROWS)
                lefts.append(by_upper(block, upper_row, uppers))
                rights.append(one_hot(low_of_row, spread(lower, s, POINT_LOW)))
        return contract(jnp.concatenate(lefts, axis=1), jnp.concatenate(rights, axis=1))

    @pl.loop(0, groups // (CHUNK * PLACES))
    def _(step):
        for place in range(PLACES):
            added = chunk((step * PLACES + place) * CHUNK, place)
            for half in range(2):
                sums[half] += added[:, half * LANES : (half + 1) * LANES]

    for half in range(2):
        total = []
        for term in range(9):
            pieces = [
                sums[half, pl.ds(part * 9 + term, uppers, stride=TERM_ROWS), :]
                for part in range(PARTS)
            ]
            total.append(pieces[0] + (pieces[1] + pieces[2]))
        solved = solve_points(total[:3], total[3:], damping[pl.ds(half, uppers, stride=2), :])
        for a in range(3):
            for h in range(uppers):
                row = ((a * 2 + half) * uppers + h) * GROUP
                answers[row : row + GROUP, :] = jnp.broadcast_to(
                    solved[a][h : h + 1, :], (GROUP, LANES)
                )

    @pl.loop(0, groups // WIDE)
    def _(step):
        bases = [(step * WIDE + w) * rows for w in range(WIDE)]
        ids = [
            received[pl.ds(base + 7, GROUP, stride=SLOT_ROWS), :].astype(i32) for base in bases
        ]
        lanes = [value & (LANES - 1) for value in ids]
        chunks = [value // LANES for value in ids]
        got = [[None] * 3 for _ in range(WIDE)]
        for w in range(WIDE):
            for a in range(3):
                for k in range(2 * uppers):
                    row = ((a * 2 + k % 2) * uppers + k // 2) * GROUP
                    value = lookup(answers[row : row + GROUP, :], lanes[w])
                    got[w][a] = value if k == 0 else jnp.where(chunks[w] == k, value, got[w][a])
        for w, base in enumerate(bases):
            rows_of = [received[pl.ds(base + r, GROUP, stride=SLOT_ROWS), :] for r in range(7)]
            y = got[w]
            images = [
                rows_of[0] * y[0] + (rows_of[1] * y[1] + rows_of[2] * y[2]),
                rows_of[3] * y[1] + rows_of[4] * y[2],
            ]
            for r in range(2):
                remain[pl.ds((step * WIDE + w) * 2 * GROUP + r, GROUP, stride=2), :] = (
                    rows_of[5 + r] - images[r]
                )


def camera_kernel(places, turns, remain, cam_jac, cam_ids, image, terms, stage):
    tiles = cam_ids.shape[0]
    copies = image.shape[0] // 18
    low_of_row = lax.broadcasted_iota(i32, (LANES, LANES), 0).astype(bf16)
    chosen = places[...].astype(bf16)
    for r in range(2):
        high, middle, low = [
            lax.dot_general(
                chosen, piece.astype(bf16), (((1,), (0,)), ((), ())), preferred_element_type=f32
            )
            for piece in split(remain[pl.ds(r, places.shape[1], stride=2), :])
        ]
        stage[r] = high + (middle + low)
    total = None
    for start in range(0, tiles // GROUP, CAM_CHUNK):
        lefts, rights = [], []
        for group in range(start, start + CAM_CHUNK):
            span = slice(group * GROUP, (group + 1) * GROUP)
            cosine, sine = turns[0, span, :], turns[1, span, :]
            rest = turn(cosine, -sine, stage[0, span, :], stage[1, span, :])
            values = [
                cam_jac[j, span, :] * rest[0] + cam_jac[9 + j, span, :] * rest[1] for j in range(9)
            ]
            store_terms(terms, values, group)
            ids = cam_ids[span, :]
            upper = (ids // LANES).astype(f32)
            lower = (ids & (LANES - 1)).astype(f32)
            for s in range(GROUP):
                block = slot_terms(terms, group, s)
                lefts.append(by_upper(block, spread(upper, s, TERM_ROWS), 2))
                rights.append(one_hot(low_of_row, spread(lower, s, LANES)))
        added = contract(jnp.concatenate(lefts, axis=1), jnp.concatenate(rights, axis=1))
        total = added if total is None else total + added
    for half in range(2):
        terms[0:TERM_ROWS, :] = total[half * TERM_ROWS : (half + 1) * TERM_ROWS, :]
        summed = terms[0:9, :] + (terms[9:18, :] + terms[18:27, :])
        for copy in range(copies):
            image[copy * 18 + half * 9 : copy * 18 + half * 9 + 9, :] = summed


def apply_blocks(precond, vector):
    total = None
    for j in range(9):
        term = precond[9 * j : 9 * j + 9, :] * vector[j : j + 1, :]
        total = term if total is None else total + term
    return total


def scalar_kernel(received, residual, direction, damping, precond, image, first_z, slope, scalars):
    copies = received.shape[0] // 18
    for half in range(2):
        columns = slice(half * LANES, (half + 1) * LANES)
        total = received[half * 9 : half * 9 + 9, :]
        for copy in range(1, copies):
            total = total + received[copy * 18 + half * 9 : copy * 18 + half * 9 + 9, :]
        image[:, columns] = damping[:, columns] * direction[:, columns] + total
    z = apply_blocks(precond, residual)
    y = apply_blocks(precond, image)
    first_z[...] = z
    slope[...] = y
    res = residual[...]
    img = image[...]
    sums = [
        jnp.sum(res * z),
        jnp.sum(direction[...] * img),
        jnp.sum(img * z + res * y),
        jnp.sum(img * y),
    ]
    lane = lax.broadcasted_iota(i32, scalars.shape, 1)
    row = jnp.zeros(scalars.shape, f32)
    for k, value in enumerate(sums):
        row = jnp.where(lane == k, value, row)
    scalars[...] = row


def final_kernel(
    scalars,
    solution_in,
    residual,
    direction,
    image,
    first_z,
    slope,
    new_solution,
    new_residual,
    new_direction,
):
    total = jnp.sum(scalars[...], axis=0, keepdims=True)
    lane = lax.broadcasted_iota(i32, total.shape, 1)
    rz, pq, cross, square = [
        jnp.sum(jnp.where(lane == k, total, 0.0), axis=1, keepdims=True) for k in range(4)
    ]
    alpha = rz / pq
    rz1 = rz + alpha * (alpha * square - cross)
    way = direction[...]
    new_solution[...] = solution_in[...] + alpha * way
    new_residual[...] = residual[...] - alpha * image[...]
    new_direction[...] = first_z[...] - alpha * slope[...] + (rz1 / rz) * way


SMEM = pl.BlockSpec(memory_space=pltpu.SMEM)
VMEM = pl.BlockSpec(memory_space=pltpu.VMEM)
LIMIT = pltpu.CompilerParams(vmem_limit_bytes=32 * 1024 * 1024)


def shape(*dims, dtype=f32):
    return jax.ShapeDtypeStruct(dims, dtype)


def pack(owners, counts, direction, cam_ids, cam_jac, pt_jac, point_ids, owner_count):
    tiles = cam_ids.shape[0]
    inputs = (owners, counts, direction, cam_ids, cam_jac, pt_jac, point_ids)
    spaces = [pltpu.SMEM] * 2 + [pltpu.VMEM] * 5
    return pl.pallas_call(
        pack_kernel,
        out_shape=(
            pltpu.VMEM((owner_count * PER_OWNER * SLOT_ROWS, LANES), f32),
            pltpu.VMEM((tiles, owner_count * PER_OWNER), f32),
            pltpu.VMEM((2, tiles, LANES), f32),
        ),
        in_specs=[pl.BlockSpec(memory_space=pltpu.HBM)] * 7,
        out_specs=(VMEM,) * 3,
        scratch_shapes=[
            pltpu.SMEM((owner_count,), i32),
            pltpu.VMEM((tiles * SLOT_ROWS, LANES), f32),
        ]
        + [space(value.shape, value.dtype) for space, value in zip(spaces, inputs)]
        + [pltpu.SemaphoreType.DMA((7,))],
        compiler_params=pltpu.CompilerParams(vmem_limit_bytes=60 * 1024 * 1024),
        name="pack_tiles",
    )(*inputs)


def points(received, damping):
    slots = received.shape[0] // SLOT_ROWS
    uppers = damping.shape[0] // 2
    return pl.pallas_call(
        point_kernel,
        out_shape=shape(slots * 2, LANES),
        in_specs=[VMEM] * 2,
        out_specs=VMEM,
        scratch_shapes=[
            pltpu.VMEM((PLACES * CHUNK * GROUP * TERM_ROWS, LANES), f32),
            pltpu.VMEM((2, uppers * TERM_ROWS, LANES), f32),
            pltpu.VMEM((6 * uppers * GROUP, LANES), f32),
        ],
        compiler_params=LIMIT,
        name="solve_points",
    )(received, damping)


def cameras(places, turns, remain, cam_jac, cam_ids, copies):
    tiles = cam_ids.shape[0]
    return pl.pallas_call(
        camera_kernel,
        out_shape=shape(copies * 18, LANES),
        in_specs=[VMEM] * 5,
        out_specs=VMEM,
        scratch_shapes=[
            pltpu.VMEM((tiles * TERM_ROWS, LANES), f32),
            pltpu.VMEM((2, tiles, LANES), f32),
        ],
        compiler_params=LIMIT,
        name="sum_cameras",
    )(places, turns, remain, cam_jac, cam_ids)


def scalar_sums(received, residual, direction, damping, precond, owner_count):
    vector = shape(*residual.shape)
    return pl.pallas_call(
        scalar_kernel,
        out_shape=(vector, vector, vector, shape(owner_count, LANES)),
        in_specs=[VMEM] * 5,
        out_specs=(VMEM,) * 4,
        compiler_params=LIMIT,
        name="camera_scalars",
    )(received, residual, direction, damping, precond)


def finish(scalars, solution_in, residual, direction, image, first_z, slope):
    vector = shape(*residual.shape)
    return pl.pallas_call(
        final_kernel,
        out_shape=(vector,) * 3,
        in_specs=[VMEM] * 7,
        out_specs=(VMEM,) * 3,
        compiler_params=LIMIT,
        name="update_vectors",
    )(scalars, solution_in, residual, direction, image, first_z, slope)


def exchange(rows, axis, count):
    depth = rows.shape[0] // count
    sent = rows.reshape(count, depth, 1, LANES)
    got = lax.all_to_all(sent, axis, split_axis=0, concat_axis=0, tiled=True)
    return got.reshape(count * depth, LANES)


def body(
    solution,
    residual,
    direction,
    cam_damping,
    precond,
    pt_damping,
    cam_jac,
    pt_jac,
    cam_ids,
    point_ids,
    owners,
    valid_counts,
):
    owner_count = lax.axis_size("cam")
    copies = lax.axis_size("pt")
    cam_jac = cam_jac.transpose(1, 0, 2)
    pt_jac = pt_jac.transpose(1, 0, 2)
    payload, places, turns = pack(
        owners.reshape(-1),
        valid_counts,
        direction,
        cam_ids,
        cam_jac,
        pt_jac,
        point_ids,
        owner_count,
    )
    received = exchange(payload, "cam", owner_count)
    remain = points(received, pt_damping.reshape(-1, LANES))
    returned = exchange(remain, "cam", owner_count)
    image_rows = cameras(places, turns, returned, cam_jac, cam_ids, copies)
    image_all = exchange(image_rows, "pt", copies)
    image, first_z, slope, scalars = scalar_sums(
        image_all, residual, direction, cam_damping, precond, owner_count
    )
    scalars_all = exchange(scalars, "cam", owner_count)
    return finish(scalars_all, solution, residual, direction, image, first_z, slope)


def solution(mesh):
    return jax.shard_map(
        body,
        mesh=mesh,
        in_specs=(
            P(None, "cam"),
            P(None, "cam"),
            P(None, "cam"),
            P(None, "cam"),
            P(None, "cam"),
            P(("cam", "pt")),
            P(("cam", "pt"), None, None),
            P(("cam", "pt"), None, None),
            P(("cam", "pt"), None),
            P(("cam", "pt"), None),
            P(("cam", "pt"), None),
            P(("cam", "pt")),
        ),
        out_specs=(P(None, "cam"), P(None, "cam"), P(None, "cam")),
        check_vma=False,
    )
```

```python
import functools

import jax
import jax.numpy as jnp
from jax import lax
from jax.experimental import pallas as pl
from jax.experimental.pallas import tpu as pltpu
from jax.sharding import PartitionSpec as P

LANES = 128
PER_OWNER = 2
SLOT_ROWS = 8
TERM_ROWS = 32
GROUP = 8
POINT_LOW = 256
PARTS = 3
CHUNK = 4
CAM_CHUNK = 2

f32 = jnp.float32
bf16 = jnp.bfloat16
i32 = jnp.int32


def split(value):
    high = value.astype(bf16).astype(f32)
    rest = value - high
    middle = rest.astype(bf16).astype(f32)
    low = (rest - middle).astype(bf16).astype(f32)
    return high, middle, low


def lookup(table, index):
    return jnp.take_along_axis(table, index, axis=1, mode="promise_in_bounds")


def contract(left, right):
    return lax.dot_general(left, right, (((1,), (1,)), ((), ())), preferred_element_type=f32)


def store_terms(terms, values, group):
    base = group * GROUP * TERM_ROWS
    for term, value in enumerate(values):
        for part, piece in enumerate(split(value)):
            at = base + (part * 9 + term) * GROUP
            terms[at : at + GROUP, :] = piece


def slot_terms(terms, group, s):
    rows = pl.ds(group * GROUP * TERM_ROWS + s, TERM_ROWS, stride=GROUP)
    return terms[rows, :].astype(bf16)


def one_hot(row_index, ids):
    return jnp.where(row_index == ids, jnp.ones((), bf16), jnp.zeros((), bf16))


def by_upper(block, upper_row, uppers):
    zero = jnp.zeros_like(block)
    return jnp.concatenate(
        [jnp.where(upper_row == jnp.asarray(h, bf16), block, zero) for h in range(uppers)], axis=0
    )


def spread(value, s, rows):
    return jnp.broadcast_to(value[s : s + 1, :], (rows, LANES)).astype(bf16)


def turn_of(first, second):
    largest = jnp.maximum(jnp.abs(first), jnp.abs(second))
    zero = largest == 0.0
    scale = jnp.where(zero, 1.0, largest)
    along = jnp.where(zero, 1.0, first / scale)
    across = second / scale
    root = jnp.sqrt(along * along + across * across)
    return along / root, across / root, largest * root


def turn(cosine, sine, first, second):
    return cosine * first + sine * second, cosine * second - sine * first


def pack_kernel(*refs):
    sources, outputs, held, sem = refs[:7], refs[7:10], refs[12:19], refs[19]
    payload, places, turns = outputs
    seen, stage = refs[10:12]
    copies = [
        pltpu.make_async_copy(source, target, sem.at[k])
        for k, (source, target) in enumerate(zip(sources, held))
    ]
    for copy in copies:
        copy.start()
    payload[...] = jnp.zeros(payload.shape, f32)
    owners, counts, direction, cam_ids, cam_jac, pt_jac, point_ids = held
    tiles = cam_ids.shape[0]
    for index in range(seen.shape[0]):
        seen[index] = 0
    for copy in copies:
        copy.wait()
    lane = lax.broadcasted_iota(i32, (GROUP, LANES), 1)
    row = lax.broadcasted_iota(i32, (GROUP, LANES), 0)
    for group in range(tiles // GROUP):
        span = slice(group * GROUP, (group + 1) * GROUP)
        ids = cam_ids[span, :]
        low = ids & (LANES - 1)
        upper = ids >= LANES
        errors = [None, None]
        for j in range(9):
            tables = [
                jnp.broadcast_to(direction[j : j + 1, LANES * c : LANES * (c + 1)], (GROUP, LANES))
                for c in range(2)
            ]
            picked = jnp.where(upper, lookup(tables[1], low), lookup(tables[0], low))
            for r in range(2):
                term = cam_jac[9 * r + j, span, :] * picked
                errors[r] = term if errors[r] is None else errors[r] + term
        used = jnp.zeros((GROUP, LANES), i32)
        for s in range(GROUP):
            used = jnp.where(row == s, counts[group * GROUP + s], used)
        valid = lane < used
        jac = [jnp.where(valid, pt_jac[a, span, :], 0.0) for a in range(6)]
        errors = [jnp.where(valid, value, 0.0) for value in errors]
        cosine, sine, length = turn_of(jac[0], jac[3])
        turns[0, span, :] = cosine
        turns[1, span, :] = sine
        upper_row, lower_row = zip(
            *[turn(cosine, sine, jac[a], jac[3 + a]) for a in (1, 2)],
            turn(cosine, sine, *errors),
        )
        values = [length, upper_row[0], upper_row[1], lower_row[0], lower_row[1]]
        values += [upper_row[2], lower_row[2], point_ids[span, :].astype(f32)]
        for r, value in enumerate(values):
            at = (group * SLOT_ROWS + r) * GROUP
            stage[at : at + GROUP, :] = value
    slot_lane = lax.broadcasted_iota(i32, (1, places.shape[1]), 1)
    for tile in range(tiles):
        owner = owners[tile]
        rank = seen[owner]
        seen[owner] = rank + 1
        slot = owner * PER_OWNER + rank
        places[tile : tile + 1, :] = jnp.where(slot_lane == slot, 1.0, 0.0)
        at = tile // GROUP * GROUP * SLOT_ROWS + tile % GROUP
        payload[pl.ds(slot * SLOT_ROWS, SLOT_ROWS), :] = stage[
            pl.ds(at, SLOT_ROWS, stride=GROUP), :
        ]


def solve_points(rhs, normal, damping):
    upper_aa = normal[0] + damping
    upper_ab = normal[1]
    upper_ac = normal[2]
    upper_bb = normal[3] + damping
    upper_bc = normal[4]
    upper_cc = normal[5] + damping
    minor_aa = upper_bb * upper_cc - upper_bc * upper_bc
    minor_ab = upper_ac * upper_bc - upper_ab * upper_cc
    minor_ac = upper_ab * upper_bc - upper_ac * upper_bb
    minor_bb = upper_aa * upper_cc - upper_ac * upper_ac
    minor_bc = upper_ab * upper_ac - upper_aa * upper_bc
    minor_cc = upper_aa * upper_bb - upper_ab * upper_ab
    determ = upper_aa * minor_aa + upper_ab * minor_ab + upper_ac * minor_ac
    return (
        (minor_aa * rhs[0] + minor_ab * rhs[1] + minor_ac * rhs[2]) / determ,
        (minor_ab * rhs[0] + minor_bb * rhs[1] + minor_bc * rhs[2]) / determ,
        (minor_ac * rhs[0] + minor_bc * rhs[1] + minor_cc * rhs[2]) / determ,
    )


def point_kernel(received, damping, remain, terms, sums, answers):
    slots = remain.shape[0] // 2
    groups = slots // GROUP
    uppers = damping.shape[0] // 2
    rows = GROUP * SLOT_ROWS
    low_of_row = lax.broadcasted_iota(i32, (POINT_LOW, LANES), 0).astype(bf16)

    def chunk(start):
        lefts, rights = [], []
        for group in range(start, start + CHUNK):
            base = group * rows
            first = [received[pl.ds(base + r, GROUP, stride=SLOT_ROWS), :] for r in range(3)]
            second = [received[pl.ds(base + 3 + r, GROUP, stride=SLOT_ROWS), :] for r in range(2)]
            err0 = received[pl.ds(base + 5, GROUP, stride=SLOT_ROWS), :]
            err1 = received[pl.ds(base + 6, GROUP, stride=SLOT_ROWS), :]
            ids = received[pl.ds(base + 7, GROUP, stride=SLOT_ROWS), :].astype(i32)
            upper = (ids // POINT_LOW).astype(f32)
            lower = (ids & (POINT_LOW - 1)).astype(f32)
            values = [first[0] * err0]
            values += [first[a] * err0 + second[a - 1] * err1 for a in (1, 2)]
            values += [first[0] * first[a] for a in range(3)]
            for a, b in ((1, 1), (1, 2), (2, 2)):
                values.append(first[a] * first[b] + second[a - 1] * second[b - 1])
            store_terms(terms, values, group)
            for s in range(GROUP):
                block = slot_terms(terms, group, s)
                upper_row = spread(upper, s, TERM_ROWS)
                lefts.append(by_upper(block, upper_row, uppers))
                rights.append(one_hot(low_of_row, spread(lower, s, POINT_LOW)))
        return contract(jnp.concatenate(lefts, axis=1), jnp.concatenate(rights, axis=1))

    total = chunk(0)
    for start in range(CHUNK, groups, CHUNK):
        total = total + chunk(start)
    for half in range(2):
        sums[half] = total[:, half * LANES : (half + 1) * LANES]

    for half in range(2):
        total = []
        for term in range(9):
            pieces = [
                sums[half, pl.ds(part * 9 + term, uppers, stride=TERM_ROWS), :]
                for part in range(PARTS)
            ]
            total.append(pieces[0] + (pieces[1] + pieces[2]))
        solved = solve_points(total[:3], total[3:], damping[pl.ds(half, uppers, stride=2), :])
        for a in range(3):
            for h in range(uppers):
                row = ((a * 2 + half) * uppers + h) * GROUP
                answers[row : row + GROUP, :] = jnp.broadcast_to(
                    solved[a][h : h + 1, :], (GROUP, LANES)
                )

    for group in range(groups):
        base = group * rows
        row_of = [received[pl.ds(base + r, GROUP, stride=SLOT_ROWS), :] for r in range(SLOT_ROWS)]
        ids = row_of[7].astype(i32)
        lane = ids & (LANES - 1)
        chunk_of = ids // LANES
        y = []
        for a in range(3):
            for k in range(2 * uppers):
                row = ((a * 2 + k % 2) * uppers + k // 2) * GROUP
                value = lookup(answers[row : row + GROUP, :], lane)
                got = value if k == 0 else jnp.where(chunk_of == k, value, got)
            y.append(got)
        images = [
            row_of[0] * y[0] + (row_of[1] * y[1] + row_of[2] * y[2]),
            row_of[3] * y[1] + row_of[4] * y[2],
        ]
        for r in range(2):
            remain[pl.ds(group * 2 * GROUP + r, GROUP, stride=2), :] = row_of[5 + r] - images[r]


def camera_kernel(places, turns, remain, cam_jac, cam_ids, image, terms, stage):
    tiles = cam_ids.shape[0]
    copies = image.shape[0] // 18
    low_of_row = lax.broadcasted_iota(i32, (LANES, LANES), 0).astype(bf16)
    chosen = places[...].astype(bf16)
    for r in range(2):
        high, middle, low = [
            lax.dot_general(
                chosen, piece.astype(bf16), (((1,), (0,)), ((), ())), preferred_element_type=f32
            )
            for piece in split(remain[pl.ds(r, places.shape[1], stride=2), :])
        ]
        stage[r] = high + (middle + low)
    total = None
    for start in range(0, tiles // GROUP, CAM_CHUNK):
        lefts, rights = [], []
        for group in range(start, start + CAM_CHUNK):
            span = slice(group * GROUP, (group + 1) * GROUP)
            cosine, sine = turns[0, span, :], turns[1, span, :]
            rest = turn(cosine, -sine, stage[0, span, :], stage[1, span, :])
            values = [
                cam_jac[j, span, :] * rest[0] + cam_jac[9 + j, span, :] * rest[1] for j in range(9)
            ]
            store_terms(terms, values, group)
            ids = cam_ids[span, :]
            upper = (ids // LANES).astype(f32)
            lower = (ids & (LANES - 1)).astype(f32)
            for s in range(GROUP):
                block = slot_terms(terms, group, s)
                lefts.append(by_upper(block, spread(upper, s, TERM_ROWS), 2))
                rights.append(one_hot(low_of_row, spread(lower, s, LANES)))
        added = contract(jnp.concatenate(lefts, axis=1), jnp.concatenate(rights, axis=1))
        total = added if total is None else total + added
    for half in range(2):
        terms[0:TERM_ROWS, :] = total[half * TERM_ROWS : (half + 1) * TERM_ROWS, :]
        summed = terms[0:9, :] + (terms[9:18, :] + terms[18:27, :])
        for copy in range(copies):
            image[copy * 18 + half * 9 : copy * 18 + half * 9 + 9, :] = summed


def apply_blocks(precond, vector):
    total = None
    for j in range(9):
        term = precond[9 * j : 9 * j + 9, :] * vector[j : j + 1, :]
        total = term if total is None else total + term
    return total


def scalar_kernel(received, residual, direction, damping, precond, image, first_z, slope, scalars):
    copies = received.shape[0] // 18
    for half in range(2):
        columns = slice(half * LANES, (half + 1) * LANES)
        total = received[half * 9 : half * 9 + 9, :]
        for copy in range(1, copies):
            total = total + received[copy * 18 + half * 9 : copy * 18 + half * 9 + 9, :]
        image[:, columns] = damping[:, columns] * direction[:, columns] + total
    z = apply_blocks(precond, residual)
    y = apply_blocks(precond, image)
    first_z[...] = z
    slope[...] = y
    res = residual[...]
    img = image[...]
    sums = [
        jnp.sum(res * z),
        jnp.sum(direction[...] * img),
        jnp.sum(img * z + res * y),
        jnp.sum(img * y),
    ]
    lane = lax.broadcasted_iota(i32, scalars.shape, 1)
    row = jnp.zeros(scalars.shape, f32)
    for k, value in enumerate(sums):
        row = jnp.where(lane == k, value, row)
    scalars[...] = row


def final_kernel(
    scalars,
    solution_in,
    residual,
    direction,
    image,
    first_z,
    slope,
    new_solution,
    new_residual,
    new_direction,
):
    total = jnp.sum(scalars[...], axis=0, keepdims=True)
    lane = lax.broadcasted_iota(i32, total.shape, 1)
    rz, pq, cross, square = [
        jnp.sum(jnp.where(lane == k, total, 0.0), axis=1, keepdims=True) for k in range(4)
    ]
    alpha = rz / pq
    rz1 = rz + alpha * (alpha * square - cross)
    way = direction[...]
    new_solution[...] = solution_in[...] + alpha * way
    new_residual[...] = residual[...] - alpha * image[...]
    new_direction[...] = first_z[...] - alpha * slope[...] + (rz1 / rz) * way


VMEM = pl.BlockSpec(memory_space=pltpu.VMEM)
LIMIT = pltpu.CompilerParams(vmem_limit_bytes=32 * 1024 * 1024)


def shape(*dims, dtype=f32):
    return jax.ShapeDtypeStruct(dims, dtype)


def pack(owners, counts, direction, cam_ids, cam_jac, pt_jac, point_ids, owner_count):
    tiles = cam_ids.shape[0]
    inputs = (owners, counts, direction, cam_ids, cam_jac, pt_jac, point_ids)
    spaces = [pltpu.SMEM] * 2 + [pltpu.VMEM] * 5
    return pl.pallas_call(
        pack_kernel,
        out_shape=(
            pltpu.VMEM((owner_count * PER_OWNER * SLOT_ROWS, LANES), f32),
            pltpu.VMEM((tiles, owner_count * PER_OWNER), f32),
            pltpu.VMEM((2, tiles, LANES), f32),
        ),
        in_specs=[pl.BlockSpec(memory_space=pltpu.HBM)] * 7,
        out_specs=(VMEM,) * 3,
        scratch_shapes=[
            pltpu.SMEM((owner_count,), i32),
            pltpu.VMEM((tiles * SLOT_ROWS, LANES), f32),
        ]
        + [space(value.shape, value.dtype) for space, value in zip(spaces, inputs)]
        + [pltpu.SemaphoreType.DMA((7,))],
        compiler_params=pltpu.CompilerParams(vmem_limit_bytes=60 * 1024 * 1024),
        name="pack_tiles",
    )(*inputs)


def points(received, damping):
    slots = received.shape[0] // SLOT_ROWS
    uppers = damping.shape[0] // 2
    return pl.pallas_call(
        point_kernel,
        out_shape=shape(slots * 2, LANES),
        in_specs=[VMEM] * 2,
        out_specs=VMEM,
        scratch_shapes=[
            pltpu.VMEM((slots * TERM_ROWS, LANES), f32),
            pltpu.VMEM((2, uppers * TERM_ROWS, LANES), f32),
            pltpu.VMEM((6 * uppers * GROUP, LANES), f32),
        ],
        compiler_params=LIMIT,
        name="solve_points",
    )(received, damping)


def cameras(places, turns, remain, cam_jac, cam_ids, copies):
    tiles = cam_ids.shape[0]
    return pl.pallas_call(
        camera_kernel,
        out_shape=shape(copies * 18, LANES),
        in_specs=[VMEM] * 5,
        out_specs=VMEM,
        scratch_shapes=[
            pltpu.VMEM((tiles * TERM_ROWS, LANES), f32),
            pltpu.VMEM((2, tiles, LANES), f32),
        ],
        compiler_params=LIMIT,
        name="sum_cameras",
    )(places, turns, remain, cam_jac, cam_ids)


def scalar_sums(received, residual, direction, damping, precond, owner_count):
    vector = shape(*residual.shape)
    return pl.pallas_call(
        scalar_kernel,
        out_shape=(vector, vector, vector, shape(owner_count, LANES)),
        in_specs=[VMEM] * 5,
        out_specs=(VMEM,) * 4,
        compiler_params=LIMIT,
        name="camera_scalars",
    )(received, residual, direction, damping, precond)


def finish(scalars, solution_in, residual, direction, image, first_z, slope):
    vector = shape(*residual.shape)
    return pl.pallas_call(
        final_kernel,
        out_shape=(vector,) * 3,
        in_specs=[VMEM] * 7,
        out_specs=(VMEM,) * 3,
        compiler_params=LIMIT,
        name="update_vectors",
    )(scalars, solution_in, residual, direction, image, first_z, slope)


def exchange(rows, axis, count):
    depth = rows.shape[0] // count
    sent = rows.reshape(count, depth, 1, LANES)
    got = lax.all_to_all(sent, axis, split_axis=0, concat_axis=0, tiled=True)
    return got.reshape(count * depth, LANES)


def body(
    solution,
    residual,
    direction,
    cam_damping,
    precond,
    pt_damping,
    cam_jac,
    pt_jac,
    cam_ids,
    point_ids,
    owners,
    valid_counts,
):
    owner_count = lax.axis_size("cam")
    copies = lax.axis_size("pt")
    cam_jac = cam_jac.transpose(1, 0, 2)
    pt_jac = pt_jac.transpose(1, 0, 2)
    payload, places, turns = pack(
        owners.reshape(-1),
        valid_counts,
        direction,
        cam_ids,
        cam_jac,
        pt_jac,
        point_ids,
        owner_count,
    )
    received = exchange(payload, "cam", owner_count)
    remain = points(received, pt_damping.reshape(-1, LANES))
    returned = exchange(remain, "cam", owner_count)
    image_rows = cameras(places, turns, returned, cam_jac, cam_ids, copies)
    image_all = exchange(image_rows, "pt", copies)
    image, first_z, slope, scalars = scalar_sums(
        image_all, residual, direction, cam_damping, precond, owner_count
    )
    scalars_all = exchange(scalars, "cam", owner_count)
    return finish(scalars_all, solution, residual, direction, image, first_z, slope)


def solution(mesh):
    return jax.shard_map(
        body,
        mesh=mesh,
        in_specs=(
            P(None, "cam"),
            P(None, "cam"),
            P(None, "cam"),
            P(None, "cam"),
            P(None, "cam"),
            P(("cam", "pt")),
            P(("cam", "pt"), None, None),
            P(("cam", "pt"), None, None),
            P(("cam", "pt"), None),
            P(("cam", "pt"), None),
            P(("cam", "pt"), None),
            P(("cam", "pt")),
        ),
        out_specs=(P(None, "cam"), P(None, "cam"), P(None, "cam")),
        check_vma=False,
    )
```

```python
import functools

import jax
import jax.numpy as jnp
from jax import lax
from jax.experimental import pallas as pl
from jax.experimental.pallas import tpu as pltpu
from jax.sharding import PartitionSpec as P

LANES = 128
PER_OWNER = 2
SLOT_ROWS = 8
TERM_ROWS = 32
GROUP = 8
POINT_LOW = 256
PARTS = 3
PIECES = 2
CHUNK = 4
CAM_CHUNK = 2

f32 = jnp.float32
bf16 = jnp.bfloat16
i32 = jnp.int32


def split(value):
    high = value.astype(bf16).astype(f32)
    rest = value - high
    middle = rest.astype(bf16).astype(f32)
    low = (rest - middle).astype(bf16).astype(f32)
    return high, middle, low


def lookup(table, index):
    return jnp.take_along_axis(table, index, axis=1, mode="promise_in_bounds")


def contract(left, right):
    return lax.dot_general(left, right, (((1,), (1,)), ((), ())), preferred_element_type=f32)


def store_terms(terms, values, group):
    base = group * GROUP * TERM_ROWS
    for term, value in enumerate(values):
        for part, piece in enumerate(split(value)):
            at = base + (part * 9 + term) * GROUP
            terms[at : at + GROUP, :] = piece


def slot_terms(terms, group, s):
    rows = pl.ds(group * GROUP * TERM_ROWS + s, TERM_ROWS, stride=GROUP)
    return terms[rows, :].astype(bf16)


def one_hot(row_index, ids):
    return jnp.where(row_index == ids, jnp.ones((), bf16), jnp.zeros((), bf16))


def by_upper(block, upper_row, uppers):
    zero = jnp.zeros_like(block)
    return jnp.concatenate(
        [jnp.where(upper_row == jnp.asarray(h, bf16), block, zero) for h in range(uppers)], axis=0
    )


def spread(value, s, rows):
    return jnp.broadcast_to(value[s : s + 1, :], (rows, LANES)).astype(bf16)


def turn_of(first, second):
    largest = jnp.maximum(jnp.abs(first), jnp.abs(second))
    zero = largest == 0.0
    scale = jnp.where(zero, 1.0, largest)
    along = jnp.where(zero, 1.0, first / scale)
    across = second / scale
    root = jnp.sqrt(along * along + across * across)
    return along / root, across / root, largest * root


def turn(cosine, sine, first, second):
    return cosine * first + sine * second, cosine * second - sine * first


def pack_kernel(*refs):
    sources, outputs, held, sem = refs[:7], refs[7:10], refs[12:19], refs[19]
    payload, places, turns = outputs
    seen, stage = refs[10:12]
    copies = [
        pltpu.make_async_copy(source, target, sem.at[k])
        for k, (source, target) in enumerate(zip(sources, held))
    ]
    for copy in copies:
        copy.start()
    payload[...] = jnp.zeros(payload.shape, f32)
    owners, counts, direction, cam_ids, cam_jac, pt_jac, point_ids = held
    tiles = cam_ids.shape[0]
    for index in range(seen.shape[0]):
        seen[index] = 0
    for copy in copies:
        copy.wait()
    lane = lax.broadcasted_iota(i32, (GROUP, LANES), 1)
    row = lax.broadcasted_iota(i32, (GROUP, LANES), 0)
    for group in range(tiles // GROUP):
        span = slice(group * GROUP, (group + 1) * GROUP)
        ids = cam_ids[span, :]
        low = ids & (LANES - 1)
        upper = ids >= LANES
        errors = [None, None]
        for j in range(9):
            tables = [
                jnp.broadcast_to(direction[j : j + 1, LANES * c : LANES * (c + 1)], (GROUP, LANES))
                for c in range(2)
            ]
            picked = jnp.where(upper, lookup(tables[1], low), lookup(tables[0], low))
            for r in range(2):
                term = cam_jac[9 * r + j, span, :] * picked
                errors[r] = term if errors[r] is None else errors[r] + term
        used = jnp.zeros((GROUP, LANES), i32)
        for s in range(GROUP):
            used = jnp.where(row == s, counts[group * GROUP + s], used)
        valid = lane < used
        jac = [jnp.where(valid, pt_jac[a, span, :], 0.0) for a in range(6)]
        errors = [jnp.where(valid, value, 0.0) for value in errors]
        cosine, sine, length = turn_of(jac[0], jac[3])
        turns[0, span, :] = cosine
        turns[1, span, :] = sine
        upper_row, lower_row = zip(
            *[turn(cosine, sine, jac[a], jac[3 + a]) for a in (1, 2)],
            turn(cosine, sine, *errors),
        )
        values = [length, upper_row[0], upper_row[1], lower_row[0], lower_row[1]]
        values += [upper_row[2], lower_row[2], point_ids[span, :].astype(f32)]
        for r, value in enumerate(values):
            at = (group * SLOT_ROWS + r) * GROUP
            stage[at : at + GROUP, :] = value
    slot_lane = lax.broadcasted_iota(i32, (1, places.shape[1]), 1)
    for tile in range(tiles):
        owner = owners[tile]
        rank = seen[owner]
        seen[owner] = rank + 1
        slot = owner * PER_OWNER + rank
        places[tile : tile + 1, :] = jnp.where(slot_lane == slot, 1.0, 0.0)
        at = tile // GROUP * GROUP * SLOT_ROWS + tile % GROUP
        payload[pl.ds(slot * SLOT_ROWS, SLOT_ROWS), :] = stage[
            pl.ds(at, SLOT_ROWS, stride=GROUP), :
        ]


def solve_points(rhs, normal, damping):
    upper_aa = normal[0] + damping
    upper_ab = normal[1]
    upper_ac = normal[2]
    upper_bb = normal[3] + damping
    upper_bc = normal[4]
    upper_cc = normal[5] + damping
    minor_aa = upper_bb * upper_cc - upper_bc * upper_bc
    minor_ab = upper_ac * upper_bc - upper_ab * upper_cc
    minor_ac = upper_ab * upper_bc - upper_ac * upper_bb
    minor_bb = upper_aa * upper_cc - upper_ac * upper_ac
    minor_bc = upper_ab * upper_ac - upper_aa * upper_bc
    minor_cc = upper_aa * upper_bb - upper_ab * upper_ab
    determ = upper_aa * minor_aa + upper_ab * minor_ab + upper_ac * minor_ac
    return (
        (minor_aa * rhs[0] + minor_ab * rhs[1] + minor_ac * rhs[2]) / determ,
        (minor_ab * rhs[0] + minor_bb * rhs[1] + minor_bc * rhs[2]) / determ,
        (minor_ac * rhs[0] + minor_bc * rhs[1] + minor_cc * rhs[2]) / determ,
    )


def point_kernel(received, damping, remain, terms, turned, answers):
    slots = remain.shape[0] // 2
    groups = slots // GROUP
    uppers = damping.shape[0] // 2
    rows = GROUP * SLOT_ROWS
    low_of_lane = lax.broadcasted_iota(i32, (LANES, POINT_LOW), 1).astype(bf16)
    upper_of_row = lax.broadcasted_iota(i32, (uppers, LANES), 0)
    ids_of = [
        received[pl.ds(group * rows + 7, GROUP, stride=SLOT_ROWS), :].astype(i32)
        for group in range(groups)
    ]
    lows = jnp.concatenate([(ids & (POINT_LOW - 1)).astype(f32) for ids in ids_of], axis=0)
    turned[...] = lows.T

    def chunk(start):
        lefts, rights = [], []
        for group in range(start, start + CHUNK):
            base = group * rows
            first = [received[pl.ds(base + r, GROUP, stride=SLOT_ROWS), :] for r in range(3)]
            second = [received[pl.ds(base + 3 + r, GROUP, stride=SLOT_ROWS), :] for r in range(2)]
            err0 = received[pl.ds(base + 5, GROUP, stride=SLOT_ROWS), :]
            err1 = received[pl.ds(base + 6, GROUP, stride=SLOT_ROWS), :]
            upper = ids_of[group] // POINT_LOW
            values = [first[0] * err0]
            values += [first[a] * err0 + second[a - 1] * err1 for a in (1, 2)]
            values += [first[0] * first[a] for a in range(3)]
            for a, b in ((1, 1), (1, 2), (2, 2)):
                values.append(first[a] * first[b] + second[a - 1] * second[b - 1])
            store_terms(terms, values, group)
            for s in range(GROUP):
                mask = upper_of_row == jnp.broadcast_to(upper[s : s + 1, :], (uppers, LANES))
                pieces = []
                for r in range(9 * PIECES):
                    at = group * GROUP * TERM_ROWS + r * GROUP + s
                    pieces.append(
                        jnp.where(mask, jnp.broadcast_to(terms[at : at + 1, :], (uppers, LANES)), 0.0)
                    )
                lefts.append(jnp.concatenate(pieces, axis=0).astype(bf16))
                slot = group * GROUP + s
                column = jnp.broadcast_to(turned[:, slot : slot + 1], (LANES, LANES)).astype(bf16)
                rights.append(
                    jnp.concatenate(
                        [one_hot(low_of_lane[:, h * LANES : (h + 1) * LANES], column) for h in range(2)],
                        axis=1,
                    )
                )
        return lax.dot_general(
            jnp.concatenate(lefts, axis=1),
            jnp.concatenate(rights, axis=0),
            (((1,), (0,)), ((), ())),
            preferred_element_type=f32,
        )

    whole = chunk(0)
    for start in range(CHUNK, groups, CHUNK):
        whole = whole + chunk(start)

    for half in range(2):
        total = []
        for term in range(9):
            parts = [
                whole[(p * 9 + term) * uppers : (p * 9 + term + 1) * uppers, half * LANES : (half + 1) * LANES]
                for p in range(PIECES)
            ]
            total.append(parts[0] + sum(parts[2:], parts[1]))
        solved = solve_points(total[:3], total[3:], damping[pl.ds(half, uppers, stride=2), :])
        for a in range(3):
            for h in range(uppers):
                row = ((a * 2 + half) * uppers + h) * GROUP
                answers[row : row + GROUP, :] = jnp.broadcast_to(
                    solved[a][h : h + 1, :], (GROUP, LANES)
                )

    for group in range(groups):
        base = group * rows
        row_of = [received[pl.ds(base + r, GROUP, stride=SLOT_ROWS), :] for r in range(SLOT_ROWS)]
        ids = row_of[7].astype(i32)
        lane = ids & (LANES - 1)
        chunk_of = ids // LANES
        y = []
        for a in range(3):
            for k in range(2 * uppers):
                row = ((a * 2 + k % 2) * uppers + k // 2) * GROUP
                value = lookup(answers[row : row + GROUP, :], lane)
                got = value if k == 0 else jnp.where(chunk_of == k, value, got)
            y.append(got)
        images = [
            row_of[0] * y[0] + (row_of[1] * y[1] + row_of[2] * y[2]),
            row_of[3] * y[1] + row_of[4] * y[2],
        ]
        for r in range(2):
            remain[pl.ds(group * 2 * GROUP + r, GROUP, stride=2), :] = row_of[5 + r] - images[r]


def camera_kernel(places, turns, remain, cam_jac, cam_ids, image, terms, stage):
    tiles = cam_ids.shape[0]
    copies = image.shape[0] // 18
    low_of_row = lax.broadcasted_iota(i32, (LANES, LANES), 0).astype(bf16)
    chosen = places[...].astype(bf16)
    for r in range(2):
        high, middle, low = [
            lax.dot_general(
                chosen, piece.astype(bf16), (((1,), (0,)), ((), ())), preferred_element_type=f32
            )
            for piece in split(remain[pl.ds(r, places.shape[1], stride=2), :])
        ]
        stage[r] = high + (middle + low)
    total = None
    for start in range(0, tiles // GROUP, CAM_CHUNK):
        lefts, rights = [], []
        for group in range(start, start + CAM_CHUNK):
            span = slice(group * GROUP, (group + 1) * GROUP)
            cosine, sine = turns[0, span, :], turns[1, span, :]
            rest = turn(cosine, -sine, stage[0, span, :], stage[1, span, :])
            values = [
                cam_jac[j, span, :] * rest[0] + cam_jac[9 + j, span, :] * rest[1] for j in range(9)
            ]
            store_terms(terms, values, group)
            ids = cam_ids[span, :]
            upper = (ids // LANES).astype(f32)
            lower = (ids & (LANES - 1)).astype(f32)
            for s in range(GROUP):
                block = slot_terms(terms, group, s)
                lefts.append(by_upper(block, spread(upper, s, TERM_ROWS), 2))
                rights.append(one_hot(low_of_row, spread(lower, s, LANES)))
        added = contract(jnp.concatenate(lefts, axis=1), jnp.concatenate(rights, axis=1))
        total = added if total is None else total + added
    for half in range(2):
        terms[0:TERM_ROWS, :] = total[half * TERM_ROWS : (half + 1) * TERM_ROWS, :]
        summed = terms[0:9, :] + (terms[9:18, :] + terms[18:27, :])
        for copy in range(copies):
            image[copy * 18 + half * 9 : copy * 18 + half * 9 + 9, :] = summed


def apply_blocks(precond, vector):
    total = None
    for j in range(9):
        term = precond[9 * j : 9 * j + 9, :] * vector[j : j + 1, :]
        total = term if total is None else total + term
    return total


def scalar_kernel(received, residual, direction, damping, precond, image, first_z, slope, scalars):
    copies = received.shape[0] // 18
    for half in range(2):
        columns = slice(half * LANES, (half + 1) * LANES)
        total = received[half * 9 : half * 9 + 9, :]
        for copy in range(1, copies):
            total = total + received[copy * 18 + half * 9 : copy * 18 + half * 9 + 9, :]
        image[:, columns] = damping[:, columns] * direction[:, columns] + total
    z = apply_blocks(precond, residual)
    y = apply_blocks(precond, image)
    first_z[...] = z
    slope[...] = y
    res = residual[...]
    img = image[...]
    sums = [
        jnp.sum(res * z),
        jnp.sum(direction[...] * img),
        jnp.sum(img * z + res * y),
        jnp.sum(img * y),
    ]
    lane = lax.broadcasted_iota(i32, scalars.shape, 1)
    row = jnp.zeros(scalars.shape, f32)
    for k, value in enumerate(sums):
        row = jnp.where(lane == k, value, row)
    scalars[...] = row


def final_kernel(
    scalars,
    solution_in,
    residual,
    direction,
    image,
    first_z,
    slope,
    new_solution,
    new_residual,
    new_direction,
):
    total = jnp.sum(scalars[...], axis=0, keepdims=True)
    lane = lax.broadcasted_iota(i32, total.shape, 1)
    rz, pq, cross, square = [
        jnp.sum(jnp.where(lane == k, total, 0.0), axis=1, keepdims=True) for k in range(4)
    ]
    alpha = rz / pq
    rz1 = rz + alpha * (alpha * square - cross)
    way = direction[...]
    new_solution[...] = solution_in[...] + alpha * way
    new_residual[...] = residual[...] - alpha * image[...]
    new_direction[...] = first_z[...] - alpha * slope[...] + (rz1 / rz) * way


VMEM = pl.BlockSpec(memory_space=pltpu.VMEM)
LIMIT = pltpu.CompilerParams(vmem_limit_bytes=32 * 1024 * 1024)


def shape(*dims, dtype=f32):
    return jax.ShapeDtypeStruct(dims, dtype)


def pack(owners, counts, direction, cam_ids, cam_jac, pt_jac, point_ids, owner_count):
    tiles = cam_ids.shape[0]
    inputs = (owners, counts, direction, cam_ids, cam_jac, pt_jac, point_ids)
    spaces = [pltpu.SMEM] * 2 + [pltpu.VMEM] * 5
    return pl.pallas_call(
        pack_kernel,
        out_shape=(
            pltpu.VMEM((owner_count * PER_OWNER * SLOT_ROWS, LANES), f32),
            pltpu.VMEM((tiles, owner_count * PER_OWNER), f32),
            pltpu.VMEM((2, tiles, LANES), f32),
        ),
        in_specs=[pl.BlockSpec(memory_space=pltpu.HBM)] * 7,
        out_specs=(VMEM,) * 3,
        scratch_shapes=[
            pltpu.SMEM((owner_count,), i32),
            pltpu.VMEM((tiles * SLOT_ROWS, LANES), f32),
        ]
        + [space(value.shape, value.dtype) for space, value in zip(spaces, inputs)]
        + [pltpu.SemaphoreType.DMA((7,))],
        compiler_params=pltpu.CompilerParams(vmem_limit_bytes=60 * 1024 * 1024),
        name="pack_tiles",
    )(*inputs)


def points(received, damping):
    slots = received.shape[0] // SLOT_ROWS
    uppers = damping.shape[0] // 2
    return pl.pallas_call(
        point_kernel,
        out_shape=shape(slots * 2, LANES),
        in_specs=[VMEM] * 2,
        out_specs=VMEM,
        scratch_shapes=[
            pltpu.VMEM((slots * TERM_ROWS, LANES), f32),
            pltpu.VMEM((LANES, slots), f32),
            pltpu.VMEM((6 * uppers * GROUP, LANES), f32),
        ],
        compiler_params=LIMIT,
        name="solve_points",
    )(received, damping)


def cameras(places, turns, remain, cam_jac, cam_ids, copies):
    tiles = cam_ids.shape[0]
    return pl.pallas_call(
        camera_kernel,
        out_shape=shape(copies * 18, LANES),
        in_specs=[VMEM] * 5,
        out_specs=VMEM,
        scratch_shapes=[
            pltpu.VMEM((tiles * TERM_ROWS, LANES), f32),
            pltpu.VMEM((2, tiles, LANES), f32),
        ],
        compiler_params=LIMIT,
        name="sum_cameras",
    )(places, turns, remain, cam_jac, cam_ids)


def scalar_sums(received, residual, direction, damping, precond, owner_count):
    vector = shape(*residual.shape)
    return pl.pallas_call(
        scalar_kernel,
        out_shape=(vector, vector, vector, shape(owner_count, LANES)),
        in_specs=[VMEM] * 5,
        out_specs=(VMEM,) * 4,
        compiler_params=LIMIT,
        name="camera_scalars",
    )(received, residual, direction, damping, precond)


def finish(scalars, solution_in, residual, direction, image, first_z, slope):
    vector = shape(*residual.shape)
    return pl.pallas_call(
        final_kernel,
        out_shape=(vector,) * 3,
        in_specs=[VMEM] * 7,
        out_specs=(VMEM,) * 3,
        compiler_params=LIMIT,
        name="update_vectors",
    )(scalars, solution_in, residual, direction, image, first_z, slope)


def exchange(rows, axis, count):
    depth = rows.shape[0] // count
    sent = rows.reshape(count, depth, 1, LANES)
    got = lax.all_to_all(sent, axis, split_axis=0, concat_axis=0, tiled=True)
    return got.reshape(count * depth, LANES)


def body(
    solution,
    residual,
    direction,
    cam_damping,
    precond,
    pt_damping,
    cam_jac,
    pt_jac,
    cam_ids,
    point_ids,
    owners,
    valid_counts,
):
    owner_count = lax.axis_size("cam")
    copies = lax.axis_size("pt")
    cam_jac = cam_jac.transpose(1, 0, 2)
    pt_jac = pt_jac.transpose(1, 0, 2)
    payload, places, turns = pack(
        owners.reshape(-1),
        valid_counts,
        direction,
        cam_ids,
        cam_jac,
        pt_jac,
        point_ids,
        owner_count,
    )
    received = exchange(payload, "cam", owner_count)
    remain = points(received, pt_damping.reshape(-1, LANES))
    returned = exchange(remain, "cam", owner_count)
    image_rows = cameras(places, turns, returned, cam_jac, cam_ids, copies)
    image_all = exchange(image_rows, "pt", copies)
    image, first_z, slope, scalars = scalar_sums(
        image_all, residual, direction, cam_damping, precond, owner_count
    )
    scalars_all = exchange(scalars, "cam", owner_count)
    return finish(scalars_all, solution, residual, direction, image, first_z, slope)


def solution(mesh):
    return jax.shard_map(
        body,
        mesh=mesh,
        in_specs=(
            P(None, "cam"),
            P(None, "cam"),
            P(None, "cam"),
            P(None, "cam"),
            P(None, "cam"),
            P(("cam", "pt")),
            P(("cam", "pt"), None, None),
            P(("cam", "pt"), None, None),
            P(("cam", "pt"), None),
            P(("cam", "pt"), None),
            P(("cam", "pt"), None),
            P(("cam", "pt")),
        ),
        out_specs=(P(None, "cam"), P(None, "cam"), P(None, "cam")),
        check_vma=False,
    )
```

```python
import functools

import jax
import jax.numpy as jnp
from jax import lax
from jax.experimental import pallas as pl
from jax.experimental.pallas import tpu as pltpu
from jax.sharding import PartitionSpec as P

LANES = 128
PER_OWNER = 2
SLOT_ROWS = 8
TERM_ROWS = 32
GROUP = 8
POINT_LOW = 256
PARTS = 3
CHUNK = 4
CAM_CHUNK = 2

f32 = jnp.float32
bf16 = jnp.bfloat16
i32 = jnp.int32


def split(value):
    high = value.astype(bf16).astype(f32)
    rest = value - high
    middle = rest.astype(bf16).astype(f32)
    low = (rest - middle).astype(bf16).astype(f32)
    return high, middle, low


def lookup(table, index):
    return jnp.take_along_axis(table, index, axis=1, mode="promise_in_bounds")


def contract(left, right):
    return lax.dot_general(left, right, (((1,), (1,)), ((), ())), preferred_element_type=f32)


def store_terms(terms, values, group):
    base = group * GROUP * TERM_ROWS
    for term, value in enumerate(values):
        for part, piece in enumerate(split(value)):
            at = base + (part * 9 + term) * GROUP
            terms[at : at + GROUP, :] = piece


def slot_terms(terms, group, s):
    rows = pl.ds(group * GROUP * TERM_ROWS + s, TERM_ROWS, stride=GROUP)
    return terms[rows, :].astype(bf16)


def one_hot(row_index, ids):
    return jnp.where(row_index == ids, jnp.ones((), bf16), jnp.zeros((), bf16))


def by_upper(block, upper_row, uppers):
    zero = jnp.zeros_like(block)
    return jnp.concatenate(
        [jnp.where(upper_row == jnp.asarray(h, bf16), block, zero) for h in range(uppers)], axis=0
    )


def spread(value, s, rows):
    return jnp.broadcast_to(value[s : s + 1, :], (rows, LANES)).astype(bf16)


def turn_of(first, second):
    largest = jnp.maximum(jnp.abs(first), jnp.abs(second))
    zero = largest == 0.0
    scale = jnp.where(zero, 1.0, largest)
    along = jnp.where(zero, 1.0, first / scale)
    across = second / scale
    root = jnp.sqrt(along * along + across * across)
    return along / root, across / root, largest * root


def turn(cosine, sine, first, second):
    return cosine * first + sine * second, cosine * second - sine * first


def pack_kernel(*refs):
    sources, outputs, held, sem = refs[:7], refs[7:10], refs[12:19], refs[19]
    payload, places, turns = outputs
    seen, stage = refs[10:12]
    copies = [
        pltpu.make_async_copy(source, target, sem.at[k])
        for k, (source, target) in enumerate(zip(sources, held))
    ]
    for copy in copies:
        copy.start()
    payload[...] = jnp.zeros(payload.shape, f32)
    owners, counts, direction, cam_ids, cam_jac, pt_jac, point_ids = held
    tiles = cam_ids.shape[0]
    for index in range(seen.shape[0]):
        seen[index] = 0
    for copy in copies:
        copy.wait()
    lane = lax.broadcasted_iota(i32, (GROUP, LANES), 1)
    row = lax.broadcasted_iota(i32, (GROUP, LANES), 0)
    for group in range(tiles // GROUP):
        span = slice(group * GROUP, (group + 1) * GROUP)
        ids = cam_ids[span, :]
        low = ids & (LANES - 1)
        upper = ids >= LANES
        errors = [None, None]
        for j in range(9):
            tables = [
                jnp.broadcast_to(direction[j : j + 1, LANES * c : LANES * (c + 1)], (GROUP, LANES))
                for c in range(2)
            ]
            picked = jnp.where(upper, lookup(tables[1], low), lookup(tables[0], low))
            for r in range(2):
                term = cam_jac[9 * r + j, span, :] * picked
                errors[r] = term if errors[r] is None else errors[r] + term
        used = jnp.zeros((GROUP, LANES), i32)
        for s in range(GROUP):
            used = jnp.where(row == s, counts[group * GROUP + s], used)
        valid = lane < used
        jac = [jnp.where(valid, pt_jac[a, span, :], 0.0) for a in range(6)]
        errors = [jnp.where(valid, value, 0.0) for value in errors]
        cosine, sine, length = turn_of(jac[0], jac[3])
        turns[0, span, :] = cosine
        turns[1, span, :] = sine
        upper_row, lower_row = zip(
            *[turn(cosine, sine, jac[a], jac[3 + a]) for a in (1, 2)],
            turn(cosine, sine, *errors),
        )
        values = [length, upper_row[0], upper_row[1], lower_row[0], lower_row[1]]
        values += [upper_row[2], lower_row[2], point_ids[span, :].astype(f32)]
        for r, value in enumerate(values):
            at = (group * SLOT_ROWS + r) * GROUP
            stage[at : at + GROUP, :] = value
    slot_lane = lax.broadcasted_iota(i32, (1, places.shape[1]), 1)
    for tile in range(tiles):
        owner = owners[tile]
        rank = seen[owner]
        seen[owner] = rank + 1
        slot = owner * PER_OWNER + rank
        places[tile : tile + 1, :] = jnp.where(slot_lane == slot, 1.0, 0.0)
        at = tile // GROUP * GROUP * SLOT_ROWS + tile % GROUP
        payload[pl.ds(slot * SLOT_ROWS, SLOT_ROWS), :] = stage[
            pl.ds(at, SLOT_ROWS, stride=GROUP), :
        ]


def solve_points(rhs, normal, damping):
    upper_aa = normal[0] + damping
    upper_ab = normal[1]
    upper_ac = normal[2]
    upper_bb = normal[3] + damping
    upper_bc = normal[4]
    upper_cc = normal[5] + damping
    minor_aa = upper_bb * upper_cc - upper_bc * upper_bc
    minor_ab = upper_ac * upper_bc - upper_ab * upper_cc
    minor_ac = upper_ab * upper_bc - upper_ac * upper_bb
    minor_bb = upper_aa * upper_cc - upper_ac * upper_ac
    minor_bc = upper_ab * upper_ac - upper_aa * upper_bc
    minor_cc = upper_aa * upper_bb - upper_ab * upper_ab
    determ = upper_aa * minor_aa + upper_ab * minor_ab + upper_ac * minor_ac
    return (
        (minor_aa * rhs[0] + minor_ab * rhs[1] + minor_ac * rhs[2]) / determ,
        (minor_ab * rhs[0] + minor_bb * rhs[1] + minor_bc * rhs[2]) / determ,
        (minor_ac * rhs[0] + minor_bc * rhs[1] + minor_cc * rhs[2]) / determ,
    )


def point_kernel(received, damping, remain, terms, sums, answers):
    slots = remain.shape[0] // 2
    groups = slots // GROUP
    uppers = damping.shape[0] // 2
    rows = GROUP * SLOT_ROWS
    low_of_row = lax.broadcasted_iota(i32, (POINT_LOW, LANES), 0).astype(bf16)

    def chunk(start):
        lefts, rights = [], []
        for group in range(start, start + CHUNK):
            base = group * rows
            first = [received[pl.ds(base + r, GROUP, stride=SLOT_ROWS), :] for r in range(3)]
            second = [received[pl.ds(base + 3 + r, GROUP, stride=SLOT_ROWS), :] for r in range(2)]
            err0 = received[pl.ds(base + 5, GROUP, stride=SLOT_ROWS), :]
            err1 = received[pl.ds(base + 6, GROUP, stride=SLOT_ROWS), :]
            ids = received[pl.ds(base + 7, GROUP, stride=SLOT_ROWS), :].astype(i32)
            upper = (ids // POINT_LOW).astype(f32)
            lower = (ids & (POINT_LOW - 1)).astype(f32)
            values = [first[0] * err0]
            values += [first[a] * err0 + second[a - 1] * err1 for a in (1, 2)]
            values += [first[0] * first[a] for a in range(3)]
            for a, b in ((1, 1), (1, 2), (2, 2)):
                values.append(first[a] * first[b] + second[a - 1] * second[b - 1])
            store_terms(terms, values, group)
            for s in range(GROUP):
                block = slot_terms(terms, group, s)
                upper_row = spread(upper, s, TERM_ROWS)
                lefts.append(by_upper(block, upper_row, uppers))
                rights.append(one_hot(low_of_row, spread(lower, s, POINT_LOW)))
        return contract(jnp.concatenate(lefts, axis=1), jnp.concatenate(rights, axis=1))

    tables = {}
    total = chunk(0)
    for start in range(CHUNK, groups, CHUNK):
        total = total + chunk(start)
    for half in range(2):
        sums[half] = total[:, half * LANES : (half + 1) * LANES]

    for half in range(2):
        total = []
        for term in range(9):
            pieces = [
                sums[half, pl.ds(part * 9 + term, uppers, stride=TERM_ROWS), :]
                for part in range(PARTS)
            ]
            total.append(pieces[0] + (pieces[1] + pieces[2]))
        solved = solve_points(total[:3], total[3:], damping[pl.ds(half, uppers, stride=2), :])
        for a in range(3):
            for h in range(uppers):
                tables[a, 2 * h + half] = jnp.broadcast_to(solved[a][h : h + 1, :], (GROUP, LANES))

    for group in range(groups):
        base = group * rows
        row_of = [received[pl.ds(base + r, GROUP, stride=SLOT_ROWS), :] for r in range(SLOT_ROWS)]
        ids = row_of[7].astype(i32)
        lane = ids & (LANES - 1)
        chunk_of = ids // LANES
        y = []
        for a in range(3):
            for k in range(2 * uppers):
                value = lookup(tables[a, k], lane)
                got = value if k == 0 else jnp.where(chunk_of == k, value, got)
            y.append(got)
        images = [
            row_of[0] * y[0] + (row_of[1] * y[1] + row_of[2] * y[2]),
            row_of[3] * y[1] + row_of[4] * y[2],
        ]
        for r in range(2):
            remain[pl.ds(group * 2 * GROUP + r, GROUP, stride=2), :] = row_of[5 + r] - images[r]


def camera_kernel(places, turns, remain, cam_jac, cam_ids, image, terms, stage):
    tiles = cam_ids.shape[0]
    copies = image.shape[0] // 18
    low_of_row = lax.broadcasted_iota(i32, (LANES, LANES), 0).astype(bf16)
    chosen = places[...].astype(bf16)
    for r in range(2):
        high, middle, low = [
            lax.dot_general(
                chosen, piece.astype(bf16), (((1,), (0,)), ((), ())), preferred_element_type=f32
            )
            for piece in split(remain[pl.ds(r, places.shape[1], stride=2), :])
        ]
        stage[r] = high + (middle + low)
    total = None
    for start in range(0, tiles // GROUP, CAM_CHUNK):
        lefts, rights = [], []
        for group in range(start, start + CAM_CHUNK):
            span = slice(group * GROUP, (group + 1) * GROUP)
            cosine, sine = turns[0, span, :], turns[1, span, :]
            rest = turn(cosine, -sine, stage[0, span, :], stage[1, span, :])
            values = [
                cam_jac[j, span, :] * rest[0] + cam_jac[9 + j, span, :] * rest[1] for j in range(9)
            ]
            store_terms(terms, values, group)
            ids = cam_ids[span, :]
            upper = (ids // LANES).astype(f32)
            lower = (ids & (LANES - 1)).astype(f32)
            for s in range(GROUP):
                block = slot_terms(terms, group, s)
                lefts.append(by_upper(block, spread(upper, s, TERM_ROWS), 2))
                rights.append(one_hot(low_of_row, spread(lower, s, LANES)))
        added = contract(jnp.concatenate(lefts, axis=1), jnp.concatenate(rights, axis=1))
        total = added if total is None else total + added
    for half in range(2):
        terms[0:TERM_ROWS, :] = total[half * TERM_ROWS : (half + 1) * TERM_ROWS, :]
        summed = terms[0:9, :] + (terms[9:18, :] + terms[18:27, :])
        for copy in range(copies):
            image[copy * 18 + half * 9 : copy * 18 + half * 9 + 9, :] = summed


def apply_blocks(precond, vector):
    total = None
    for j in range(9):
        term = precond[9 * j : 9 * j + 9, :] * vector[j : j + 1, :]
        total = term if total is None else total + term
    return total


def scalar_kernel(received, residual, direction, damping, precond, image, first_z, slope, scalars):
    copies = received.shape[0] // 18
    for half in range(2):
        columns = slice(half * LANES, (half + 1) * LANES)
        total = received[half * 9 : half * 9 + 9, :]
        for copy in range(1, copies):
            total = total + received[copy * 18 + half * 9 : copy * 18 + half * 9 + 9, :]
        image[:, columns] = damping[:, columns] * direction[:, columns] + total
    z = apply_blocks(precond, residual)
    y = apply_blocks(precond, image)
    first_z[...] = z
    slope[...] = y
    res = residual[...]
    img = image[...]
    sums = [
        jnp.sum(res * z),
        jnp.sum(direction[...] * img),
        jnp.sum(img * z + res * y),
        jnp.sum(img * y),
    ]
    lane = lax.broadcasted_iota(i32, scalars.shape, 1)
    row = jnp.zeros(scalars.shape, f32)
    for k, value in enumerate(sums):
        row = jnp.where(lane == k, value, row)
    scalars[...] = row


def final_kernel(
    scalars,
    solution_in,
    residual,
    direction,
    image,
    first_z,
    slope,
    new_solution,
    new_residual,
    new_direction,
):
    total = jnp.sum(scalars[...], axis=0, keepdims=True)
    lane = lax.broadcasted_iota(i32, total.shape, 1)
    rz, pq, cross, square = [
        jnp.sum(jnp.where(lane == k, total, 0.0), axis=1, keepdims=True) for k in range(4)
    ]
    alpha = rz / pq
    rz1 = rz + alpha * (alpha * square - cross)
    way = direction[...]
    new_solution[...] = solution_in[...] + alpha * way
    new_residual[...] = residual[...] - alpha * image[...]
    new_direction[...] = first_z[...] - alpha * slope[...] + (rz1 / rz) * way


VMEM = pl.BlockSpec(memory_space=pltpu.VMEM)
LIMIT = pltpu.CompilerParams(vmem_limit_bytes=32 * 1024 * 1024)


def shape(*dims, dtype=f32):
    return jax.ShapeDtypeStruct(dims, dtype)


def pack(owners, counts, direction, cam_ids, cam_jac, pt_jac, point_ids, owner_count):
    tiles = cam_ids.shape[0]
    inputs = (owners, counts, direction, cam_ids, cam_jac, pt_jac, point_ids)
    spaces = [pltpu.SMEM] * 2 + [pltpu.VMEM] * 5
    return pl.pallas_call(
        pack_kernel,
        out_shape=(
            pltpu.VMEM((owner_count * PER_OWNER * SLOT_ROWS, LANES), f32),
            pltpu.VMEM((tiles, owner_count * PER_OWNER), f32),
            pltpu.VMEM((2, tiles, LANES), f32),
        ),
        in_specs=[pl.BlockSpec(memory_space=pltpu.HBM)] * 7,
        out_specs=(VMEM,) * 3,
        scratch_shapes=[
            pltpu.SMEM((owner_count,), i32),
            pltpu.VMEM((tiles * SLOT_ROWS, LANES), f32),
        ]
        + [space(value.shape, value.dtype) for space, value in zip(spaces, inputs)]
        + [pltpu.SemaphoreType.DMA((7,))],
        compiler_params=pltpu.CompilerParams(vmem_limit_bytes=60 * 1024 * 1024),
        name="pack_tiles",
    )(*inputs)


def points(received, damping):
    slots = received.shape[0] // SLOT_ROWS
    uppers = damping.shape[0] // 2
    return pl.pallas_call(
        point_kernel,
        out_shape=shape(slots * 2, LANES),
        in_specs=[VMEM] * 2,
        out_specs=VMEM,
        scratch_shapes=[
            pltpu.VMEM((slots * TERM_ROWS, LANES), f32),
            pltpu.VMEM((2, uppers * TERM_ROWS, LANES), f32),
            pltpu.VMEM((6 * uppers * GROUP, LANES), f32),
        ],
        compiler_params=LIMIT,
        name="solve_points",
    )(received, damping)


def cameras(places, turns, remain, cam_jac, cam_ids, copies):
    tiles = cam_ids.shape[0]
    return pl.pallas_call(
        camera_kernel,
        out_shape=shape(copies * 18, LANES),
        in_specs=[VMEM] * 5,
        out_specs=VMEM,
        scratch_shapes=[
            pltpu.VMEM((tiles * TERM_ROWS, LANES), f32),
            pltpu.VMEM((2, tiles, LANES), f32),
        ],
        compiler_params=LIMIT,
        name="sum_cameras",
    )(places, turns, remain, cam_jac, cam_ids)


def scalar_sums(received, residual, direction, damping, precond, owner_count):
    vector = shape(*residual.shape)
    return pl.pallas_call(
        scalar_kernel,
        out_shape=(vector, vector, vector, shape(owner_count, LANES)),
        in_specs=[VMEM] * 5,
        out_specs=(VMEM,) * 4,
        compiler_params=LIMIT,
        name="camera_scalars",
    )(received, residual, direction, damping, precond)


def finish(scalars, solution_in, residual, direction, image, first_z, slope):
    vector = shape(*residual.shape)
    return pl.pallas_call(
        final_kernel,
        out_shape=(vector,) * 3,
        in_specs=[VMEM] * 7,
        out_specs=(VMEM,) * 3,
        compiler_params=LIMIT,
        name="update_vectors",
    )(scalars, solution_in, residual, direction, image, first_z, slope)


def exchange(rows, axis, count):
    depth = rows.shape[0] // count
    sent = rows.reshape(count, depth, 1, LANES)
    got = lax.all_to_all(sent, axis, split_axis=0, concat_axis=0, tiled=True)
    return got.reshape(count * depth, LANES)


def body(
    solution,
    residual,
    direction,
    cam_damping,
    precond,
    pt_damping,
    cam_jac,
    pt_jac,
    cam_ids,
    point_ids,
    owners,
    valid_counts,
):
    owner_count = lax.axis_size("cam")
    copies = lax.axis_size("pt")
    cam_jac = cam_jac.transpose(1, 0, 2)
    pt_jac = pt_jac.transpose(1, 0, 2)
    payload, places, turns = pack(
        owners.reshape(-1),
        valid_counts,
        direction,
        cam_ids,
        cam_jac,
        pt_jac,
        point_ids,
        owner_count,
    )
    received = exchange(payload, "cam", owner_count)
    remain = points(received, pt_damping.reshape(-1, LANES))
    returned = exchange(remain, "cam", owner_count)
    image_rows = cameras(places, turns, returned, cam_jac, cam_ids, copies)
    image_all = exchange(image_rows, "pt", copies)
    image, first_z, slope, scalars = scalar_sums(
        image_all, residual, direction, cam_damping, precond, owner_count
    )
    scalars_all = exchange(scalars, "cam", owner_count)
    return finish(scalars_all, solution, residual, direction, image, first_z, slope)


def solution(mesh):
    return jax.shard_map(
        body,
        mesh=mesh,
        in_specs=(
            P(None, "cam"),
            P(None, "cam"),
            P(None, "cam"),
            P(None, "cam"),
            P(None, "cam"),
            P(("cam", "pt")),
            P(("cam", "pt"), None, None),
            P(("cam", "pt"), None, None),
            P(("cam", "pt"), None),
            P(("cam", "pt"), None),
            P(("cam", "pt"), None),
            P(("cam", "pt")),
        ),
        out_specs=(P(None, "cam"), P(None, "cam"), P(None, "cam")),
        check_vma=False,
    )
```
